256 devices in a mesh: ctx: 64 (over y, z, core), grp: 4 (over x).
Axes of the slice: x: 4, y: 4, z: 8, core: 2. Of those that a mesh axis runs over, the one named last changes fastest.
Arguments:
- queries: bfloat16 [65536, 1024], P(('ctx', 'grp')), may hold values from -6 to 6
- key_rows: bfloat16 [65536, 128], P(('ctx', 'grp')), may hold values from -6 to 6
- value_rows: bfloat16 [65536, 128], P(('ctx', 'grp')), may hold values from -6 to 6
- out_grad: bfloat16 [65536, 1024], P(('ctx', 'grp')), may hold values from -6 to 6
- doc_lengths: int32 [128], replicated, may hold values from 1 to 1024, 65536 in all
Outputs:
- attended: bfloat16 [65536, 1024], P(('ctx', 'grp'))
- query_grad: bfloat16 [65536, 1024], P(('ctx', 'grp'))
- key_grad: bfloat16 [65536, 128], P(('ctx', 'grp'))
- value_grad: bfloat16 [65536, 128], P(('ctx', 'grp'))
The draws below stay inside these ranges and needn't reach their ends.
Inputs may be any that keep to these rules, and one draw needn't show every extreme that they name: `doc_lengths`: the lengths sum to 65536; one document has exactly 1024 tokens.
All inputs are finite; a program needn't handle non-finite values.
Results may differ from the reference program's by a relative error of at most 0.028.
Values may be sent and summed in bfloat16 or wider, within the bound.
No kernel may reach another device: no remote copies, remote signals or barrier semaphores. Data moves between devices by JAX's collectives and lax.ppermute only.
A program may use at most 64 MiB of HBM per device.

```python
import math
import jax
import jax.numpy as jnp
import numpy as np
from jax import lax

HQ = 8
DH = 128
TOK_DEV = 256
MOST = 1024
SEQ = 65536
NDOC = 128


def draw_key_rows(key, part):
    key = jax.random.fold_in(key, 11)
    result = jnp.clip(jax.random.normal(key, (SEQ, DH), jnp.float32), -5.0, 5.0)
    return result.astype(jnp.bfloat16)


def draw_queries(key, part):
    key = jax.random.fold_in(key, 12)
    result = jnp.clip(jax.random.normal(key, (SEQ, HQ * DH), jnp.float32), -5.0, 5.0)
    return result.astype(jnp.bfloat16)


def level_of(key, shape, shards, smallest, high):
    level = 1.0
    for axis_at, shards_of in shards:
        heights = jax.random.uniform(jax.random.fold_in(jax.random.fold_in(key, 6), axis_at), (shards_of,), jnp.float32, smallest / len(shards), high / len(shards))
        level = level * jnp.repeat(jnp.exp(heights), shape[axis_at] // shards_of).reshape((-1,) + (1,) * (len(shape) - 1 - axis_at))
    return level


def split_up(count, total, reach, skew):
    loads = [(1 << 20) // math.isqrt(standing ** skew) + 1 for standing in range(2, count + 1)]
    spare, holding = total - reach - (count - 1), [1] * (count - 1)
    while spare > 0:
        free = [i for i in range(count - 1) if holding[i] < reach]
        pool, remaining = sum([loads[i] for i in free]), spare
        for i in free:
            addition = min(reach - holding[i], max(1, remaining * loads[i] // pool), spare)
            holding[i] = holding[i] + addition
            spare = spare - addition
    return np.array([reach] + holding)


def ragged_sizes(rng, amount, total, reach, slope):
    if amount == 2:
        one = jax.random.randint(rng, (), max(1, total - reach), min(reach, total - 1) + 1)
        return jnp.stack([one, total - one])
    tallies = jnp.asarray(split_up(amount, total, reach, slope), jnp.int32)
    couples = (amount - 1) // 2
    giver, taker = tallies[1:1 + 2 * couples:2], tallies[2:2 + 2 * couples:2]
    room = jnp.minimum(giver - 1, reach - taker)
    moved = jax.random.randint(jax.random.fold_in(rng, 1), (couples,), 0, 1 << 20) % (room + 1)
    tallies = tallies.at[1:1 + 2 * couples:2].set(giver - moved).at[2:2 + 2 * couples:2].set(taker + moved)
    return tallies[jax.random.permutation(jax.random.fold_in(rng, 2), amount)]


def normal_values(rng, dims, deviation, limit, cuts=(), kind=jnp.bfloat16):
    values = deviation * jax.random.normal(rng, dims, jnp.float32)
    if cuts:
        values = values * level_of(rng, dims, cuts, -0.22, 0.18)
    return jnp.clip(values, -limit, limit).astype(kind)


def setup_inputs(seed: int = 0) -> dict:
    keys = jax.random.split(jax.random.key(seed), 6)
    queries = draw_queries(jax.random.fold_in(keys[5], 71), 0)
    key_rows = draw_key_rows(jax.random.fold_in(keys[5], 71), 0)
    value_rows = normal_values(keys[2], (SEQ, DH), 1.0, 6.0, ((0, 256),))
    out_grad = normal_values(keys[3], (SEQ, HQ * DH), 1.0, 6.0, ((0, 256),))
    doc_lengths = ragged_sizes(keys[4], NDOC, SEQ, MOST, 2).astype(jnp.int32)
    return {"queries": queries, "key_rows": key_rows, "value_rows": value_rows, "out_grad": out_grad, "doc_lengths": doc_lengths}


def window_attention(query_part, window, grad_part, query_first, key_first, doc_start):
    row_count = query_part.shape[0]
    width = window.shape[0]
    head_dim = window.shape[1] // 2
    heads = query_part.shape[1] // head_dim
    keys_win = window[:, :head_dim]
    values_win = window[:, head_dim:]
    factor = 1.0 / math.sqrt(head_dim)
    step_rows = min(128, row_count)
    key_pos = key_first + jnp.arange(width, dtype=jnp.int32)
    grad_window = jnp.zeros((width, 2 * head_dim), jnp.float32)
    outputs = []
    qgrads = []
    for block_index in range(row_count // step_rows):
        low = block_index * step_rows
        query_pos = query_first + low + jnp.arange(step_rows, dtype=jnp.int32)
        begins = lax.optimization_barrier(jnp.max(jnp.where(doc_start[None, :] <= query_pos[:, None], doc_start[None, :], 0), axis=1)).astype(jnp.int32)
        visible = (key_pos[None, :] >= begins[:, None]) & (key_pos[None, :] <= query_pos[:, None])
        mask_three = visible[:, None, :]
        query_flat = query_part[low:low + step_rows].reshape(step_rows * heads, head_dim)
        grad_flat = grad_part[low:low + step_rows].reshape(step_rows * heads, head_dim)
        scores = lax.dot_general(query_flat, keys_win, (((1,), (1,)), ((), ())), preferred_element_type=jnp.float32)
        scores = scores.reshape(step_rows, heads, width) * factor
        highest = lax.optimization_barrier(jnp.max(jnp.where(mask_three, scores, -jnp.inf), axis=2, keepdims=True))
        weights = jnp.exp(jnp.where(mask_three, scores - highest, -jnp.inf))
        denom = lax.optimization_barrier(jnp.sum(weights, axis=2, keepdims=True))
        probs = (weights / denom).reshape(step_rows * heads, width)
        probs_low = probs.astype(jnp.bfloat16)
        output_low = jnp.dot(probs_low, values_win, preferred_element_type=jnp.float32).astype(jnp.bfloat16)
        dprobs = lax.dot_general(grad_flat, values_win, (((1,), (1,)), ((), ())), preferred_element_type=jnp.float32)
        deltas = lax.optimization_barrier(jnp.sum(grad_flat.astype(jnp.float32) * output_low.astype(jnp.float32), axis=1, keepdims=True))
        dscores = (probs * (dprobs - deltas) * factor).astype(jnp.bfloat16)
        qgrad_low = jnp.dot(dscores, keys_win, preferred_element_type=jnp.float32).astype(jnp.bfloat16)
        key_part = lax.dot_general(dscores, query_flat, (((0,), (0,)), ((), ())), preferred_element_type=jnp.float32)
        value_part = lax.dot_general(probs_low, grad_flat, (((0,), (0,)), ((), ())), preferred_element_type=jnp.float32)
        grad_window = grad_window + jnp.concatenate([key_part, value_part], axis=1)
        outputs.append(output_low.reshape(step_rows, heads * head_dim))
        qgrads.append(qgrad_low.reshape(step_rows, heads * head_dim))
    return (jnp.concatenate(outputs, axis=0), jnp.concatenate(qgrads, axis=0), grad_window)

def starts_of(doc_lengths):
    lengths_int = doc_lengths.astype(jnp.int32)
    return (jnp.cumsum(lengths_int).astype(jnp.int32) - lengths_int).astype(jnp.int32)

def reference(queries, key_rows, value_rows, out_grad, doc_lengths):
    doc_start = starts_of(doc_lengths)
    packed = jnp.concatenate([key_rows, value_rows], axis=1)
    padded = jnp.concatenate([jnp.zeros((MOST, 2 * DH), jnp.bfloat16), packed], axis=0)

    def advance(carry, block_index):
        first = (block_index * TOK_DEV).astype(jnp.int32)
        query_part = lax.dynamic_slice_in_dim(queries, first, TOK_DEV, 0)
        grad_part = lax.dynamic_slice_in_dim(out_grad, first, TOK_DEV, 0)
        window = lax.dynamic_slice_in_dim(padded, first, MOST + TOK_DEV, 0)
        output_part, qgrad_part, grad_window = window_attention(query_part, window, grad_part, first, first - MOST, doc_start)
        before = lax.dynamic_slice_in_dim(carry, first, MOST + TOK_DEV, 0)
        carry = lax.dynamic_update_slice_in_dim(carry, before + grad_window, first, 0)
        return (carry, (output_part, qgrad_part))
    carry, (outputs, qgrads) = lax.scan(advance, jnp.zeros((SEQ + MOST, 2 * DH), jnp.float32), jnp.arange(SEQ // TOK_DEV, dtype=jnp.int32))
    grads = carry[MOST:]
    return (outputs.reshape(SEQ, HQ * DH), qgrads.reshape(SEQ, HQ * DH), grads[:, :DH].astype(jnp.bfloat16), grads[:, DH:].astype(jnp.bfloat16))
```

```python
import functools, math
import jax
import jax.numpy as jnp
from jax import lax
from jax.experimental import pallas as pl
from jax.experimental.pallas import tpu as pltpu
from jax.sharding import PartitionSpec as P

F32, BF16 = jnp.float32, jnp.bfloat16
NT = (((1,), (1,)), ((), ()))
NN = (((1,), (0,)), ((), ()))
LOG2E = 1.4426950408889634

def attention_kernel(lens_ref, q_ref, do_ref, k_ref, v_ref, *refs, first_of, unroll):
    reach = 4
    far = refs[:reach]
    out_ref, dq_ref = refs[reach:reach + 2]
    back = refs[reach + 2:2 * reach + 2]
    mine_ref, bias, s_buf, dp_buf, p_buf, ds_buf, qs, dos, vt, kt = refs[2 * reach + 2:]
    rows, hd = k_ref.shape
    heads = q_ref.shape[1] // hd
    nb = reach + 1
    width = nb * rows
    factor = 1.0 / math.sqrt(hd)
    q0 = first_of()
    nd = lens_ref.shape[1]
    lens = lens_ref[...]
    di = lax.broadcasted_iota(jnp.int32, (nd, nd), 0)
    dj = lax.broadcasted_iota(jnp.int32, (nd, nd), 1)
    ends = jnp.sum(jnp.where(dj <= di, lens, 0), axis=1, keepdims=True)
    mylen = jnp.sum(jnp.where(dj == di, lens, 0), axis=1, keepdims=True)
    qpos = q0 + lax.broadcasted_iota(jnp.int32, (1, rows), 1)
    begin = jnp.sum(jnp.where(ends <= qpos, mylen, 0), axis=0, keepdims=True)
    def kv(b):
        if b == reach:
            return k_ref[...], v_ref[...]
        return far[b][0:rows, :], far[b][rows:, :]
    for b in range(nb):
        kpos = q0 + (b - reach) * rows + lax.broadcasted_iota(jnp.int32, (rows, 1), 0)
        bias[b * rows:(b + 1) * rows, :] = jnp.where((kpos >= begin) & (kpos <= qpos), 0.0, -jnp.inf)
        k, v = kv(b)
        kt[:, b * rows:(b + 1) * rows] = k.T
        vt[:, b * rows:(b + 1) * rows] = v.T
    def head(h):
        hs = pl.ds(pl.multiple_of(h * hd, hd), hd) if not isinstance(h, int) else slice(h * hd, (h + 1) * hd)
        ps = pl.ds(pl.multiple_of(h * rows, rows), rows) if not isinstance(h, int) else slice(h * rows, (h + 1) * rows)
        q = q_ref[:, hs]
        do = do_ref[:, hs]
        qs[ps, :] = q
        dos[ps, :] = do
        m = jnp.full((8, rows), -jnp.inf, F32)
        for b in range(nb):
            bs = slice(b * rows, (b + 1) * rows)
            k, v = kv(b)
            s = lax.dot_general(k, q, NT, preferred_element_type=F32) * (factor * LOG2E) + bias[bs, :]
            s_buf[bs, :] = s
            m = jnp.maximum(m, jnp.max(s.reshape(rows // 8, 8, rows), axis=0))
            dp_buf[bs, :] = lax.dot_general(v, do, NT, preferred_element_type=F32)
        m = jnp.max(m, axis=0, keepdims=True)
        l = jnp.zeros((8, rows), F32)
        t = jnp.zeros((8, rows), F32)
        for b in range(nb):
            bs = slice(b * rows, (b + 1) * rows)
            p = jnp.exp2(s_buf[bs, :] - m)
            s_buf[bs, :] = p
            l = l + jnp.sum(p.reshape(rows // 8, 8, rows), axis=0)
            t = t + jnp.sum((p * dp_buf[bs, :]).reshape(rows // 8, 8, rows), axis=0)
        inv = 1.0 / jnp.sum(l, axis=0, keepdims=True)
        delta = jnp.sum(t, axis=0, keepdims=True) * inv
        for b in range(nb):
            bs = slice(b * rows, (b + 1) * rows)
            p = s_buf[bs, :] * inv
            p_buf[bs, ps] = p.astype(BF16)
            ds_buf[bs, ps] = (p * (dp_buf[bs, :] - delta)).astype(BF16)
        o = lax.dot_general(vt[...], p_buf[:, ps], NN, preferred_element_type=F32)
        out_ref[:, hs] = o.T.astype(BF16)
        dq = lax.dot_general(kt[...], ds_buf[:, ps], NN, preferred_element_type=F32) * factor
        dq_ref[:, hs] = dq.T.astype(BF16)
    if unroll:
        for h in range(heads):
            head(h)
    else:
        @pl.loop(0, heads)
        def _(h):
            head(h)
    for b in range(nb):
        bs = slice(b * rows, (b + 1) * rows)
        dv = lax.dot_general(p_buf[bs, :], dos[...], NN, preferred_element_type=F32)
        dk = lax.dot_general(ds_buf[bs, :], qs[...], NN, preferred_element_type=F32) * factor
        ref = mine_ref if b == reach else back[b]
        ref[0:rows, :] = dk.astype(ref.dtype)
        ref[rows:, :] = dv.astype(ref.dtype)

def attention(lens, q, do, k, v, far, first_of, unroll=False):
    rows, hd = k.shape
    reach = len(far)
    width = (reach + 1) * rows
    heads = q.shape[1] // hd
    sd = jax.ShapeDtypeStruct
    vm = pl.BlockSpec(memory_space=pltpu.VMEM)
    return pl.pallas_call(
        functools.partial(attention_kernel, first_of=first_of, unroll=unroll),
        out_shape=[sd(q.shape, BF16), sd(q.shape, BF16)] + [sd((2 * rows, hd), BF16)] * reach + [sd((2 * rows, hd), F32)],
        in_specs=[vm] * (5 + reach),
        out_specs=[vm] * (3 + reach),
        scratch_shapes=[
            pltpu.VMEM((width, rows), F32), pltpu.VMEM((width, rows), F32), pltpu.VMEM((width, rows), F32),
            pltpu.VMEM((width, heads * rows), BF16), pltpu.VMEM((width, heads * rows), BF16),
            pltpu.VMEM((heads * rows, hd), BF16), pltpu.VMEM((heads * rows, hd), BF16),
            pltpu.VMEM((hd, width), BF16), pltpu.VMEM((hd, width), BF16),
        ],
        compiler_params=pltpu.CompilerParams(vmem_limit_bytes=48 * 2**20),
        name="window",
    )(lens.reshape(1, -1), q, do, k, v, *far)


REACH = 4


def shifted(block, distance):
    count = lax.axis_size("ctx") * lax.axis_size("grp")
    route = [(i, (i + distance) % count) for i in range(count)]
    return lax.ppermute(block, ("ctx", "grp"), route)


def body(queries, key_rows, value_rows, out_grad, doc_lengths):
    rows, hd = key_rows.shape

    def first_of():
        return (lax.axis_index("ctx") * lax.axis_size("grp") + lax.axis_index("grp")) * rows

    packed = jnp.concatenate([key_rows, value_rows], axis=0)
    far = [shifted(packed, d) for d in range(REACH, 0, -1)]
    attended, query_grad, *parts = attention(
        doc_lengths, queries, out_grad, key_rows, value_rows, far, first_of, True
    )
    total = parts[-1]
    for d in range(REACH, 0, -1):
        total = total + shifted(parts[REACH - d], -d).astype(F32)
    total = total.astype(BF16)
    return attended, query_grad, total[:rows], total[rows:]


def solution(mesh):
    split = P(("ctx", "grp"), None)
    return jax.shard_map(
        body, mesh=mesh, in_specs=(split,) * 4 + (P(),), out_specs=(split,) * 4, check_vma=False
    )
```

```python
import functools
import math

import jax
import jax.numpy as jnp
from jax import lax
from jax.experimental import pallas as pl
from jax.experimental.pallas import tpu as pltpu
from jax.sharding import PartitionSpec as P

F32, BF16 = jnp.float32, jnp.bfloat16
NT = (((1,), (1,)), ((), ()))
NN = (((1,), (0,)), ((), ()))
LOG2E = 1.4426950408889634
REACH = 4
CHUNK = 64


def dot(a, b, dims):
    return lax.dot_general(a, b, dims, preferred_element_type=F32)


def fold(x, op):
    return op(x.reshape(x.shape[0] // 8, 8, x.shape[1]), axis=0)


def local_kernel(lens_ref, q_ref, do_ref, k_ref, v_ref, qs, dos, bias, st_ref, *, first_of):
    heads, rows, hd = qs.shape
    scale = LOG2E / math.sqrt(hd)
    q0 = first_of()
    nd = lens_ref.shape[1]
    lens = lens_ref[...]
    di = lax.broadcasted_iota(jnp.int32, (nd, nd), 0)
    dj = lax.broadcasted_iota(jnp.int32, (nd, nd), 1)
    ends = jnp.sum(jnp.where(dj <= di, lens, 0), axis=1, keepdims=True)
    length = jnp.sum(jnp.where(dj == di, lens, 0), axis=1, keepdims=True)
    qpos = q0 + lax.broadcasted_iota(jnp.int32, (1, rows), 1)
    begin = jnp.sum(jnp.where(ends <= qpos, length, 0), axis=0, keepdims=True)
    for b in range(REACH + 1):
        kpos = q0 + (b - REACH) * rows + lax.broadcasted_iota(jnp.int32, (rows, 1), 0)
        bias[b * rows : (b + 1) * rows, :] = jnp.where(
            (kpos >= begin) & (kpos <= qpos), 0.0, -jnp.inf
        )
    for h in range(heads):
        q = q_ref[:, h * hd : (h + 1) * hd]
        do = do_ref[:, h * hd : (h + 1) * hd]
        qs[h] = q
        dos[h] = do
        s = dot(k_ref[...], q, NT) * scale + bias[REACH * rows :, :]
        m = jnp.max(fold(s, jnp.max), axis=0, keepdims=True)
        p = jnp.exp2(s - m)
        dp = dot(v_ref[...], do, NT)
        st_ref[h, 0:1, :] = m
        st_ref[h, 1:2, :] = jnp.sum(fold(p, jnp.sum), axis=0, keepdims=True)
        st_ref[h, 2:3, :] = jnp.sum(fold(p * dp, jnp.sum), axis=0, keepdims=True)


def remote_kernel(q_ref, do_ref, bias, st_ref, *refs):
    far = refs[:REACH]
    back = refs[REACH : 2 * REACH]
    p_out, ds_out, st_out, kall, vall, s_buf, dp_buf, m_buf, dv_acc, dk_acc = refs[2 * REACH :]
    heads, rows, hd = q_ref.shape
    width = REACH * rows
    factor = 1.0 / math.sqrt(hd)
    scale = factor * LOG2E
    for b in range(REACH):
        kall[b * rows : (b + 1) * rows, :] = far[b][0:rows, :]
        vall[b * rows : (b + 1) * rows, :] = far[b][rows:, :]
    chunks = [slice(c, c + CHUNK) for c in range(0, width, CHUNK)]

    def scores(h):
        s = dot(kall[...], q_ref[h], NT)
        dp = dot(vall[...], do_ref[h], NT)
        m = jnp.full((8, rows), -jnp.inf, F32)
        for cs in chunks:
            x = s[cs, :] * scale + bias[cs, :]
            m = jnp.maximum(m, fold(x, jnp.max))
            s_buf[cs, :] = x
            dp_buf[cs, :] = dp[cs, :]
        m_buf[...] = m

    def statistics(h):
        m0 = st_ref[h, 0:1, :]
        m = jnp.maximum(m0, jnp.max(m_buf[...], axis=0, keepdims=True))
        w0 = jnp.exp2(m0 - m)
        l = jnp.zeros((8, rows), F32)
        t = jnp.zeros((8, rows), F32)
        for cs in chunks:
            p = jnp.exp2(s_buf[cs, :] - m)
            l = l + fold(p, jnp.sum)
            t = t + fold(p * dp_buf[cs, :], jnp.sum)
        total = jnp.sum(l, axis=0, keepdims=True) + w0 * st_ref[h, 1:2, :]
        delta = (jnp.sum(t, axis=0, keepdims=True) + w0 * st_ref[h, 2:3, :]) / total
        lse = m + jnp.log2(total)
        st_out[h, 0:1, :] = lse
        st_out[h, 1:2, :] = delta
        return lse, delta

    def weights(h, lse, delta):
        for cs in chunks:
            p = jnp.exp2(s_buf[cs, :] - lse)
            p_out[h, cs, :] = p.astype(BF16)
            ds_out[h, cs, :] = (p * (dp_buf[cs, :] - delta)).astype(BF16)

    def grads(h):
        dv_acc[...] += dot(p_out[h], do_ref[h], NN)
        dk_acc[...] += dot(ds_out[h], q_ref[h], NN)

    dv_acc[...] = jnp.zeros_like(dv_acc)
    dk_acc[...] = jnp.zeros_like(dk_acc)
    scores(0)
    weights(0, *statistics(0))
    scores(1)

    @pl.loop(1, heads - 1)
    def _(h):
        grads(h - 1)
        weights(h, *statistics(h))
        scores(h + 1)

    grads(heads - 2)
    weights(heads - 1, *statistics(heads - 1))
    grads(heads - 1)
    for b in range(REACH):
        bs = slice(b * rows, (b + 1) * rows)
        back[b][0:rows, :] = (dk_acc[bs, :] * factor).astype(BF16)
        back[b][rows:, :] = dv_acc[bs, :].astype(BF16)


def own_kernel(q_ref, do_ref, bias, st_ref, p_ref, ds_ref, k_ref, v_ref, *refs):
    far = refs[:REACH]
    out_ref, dq_ref, mine_ref, kt, vt = refs[REACH:]
    heads, rows, hd = q_ref.shape
    width = REACH * rows
    factor = 1.0 / math.sqrt(hd)
    scale = factor * LOG2E
    for b in range(REACH):
        kt[:, b * rows : (b + 1) * rows] = far[b][0:rows, :].T
        vt[:, b * rows : (b + 1) * rows] = far[b][rows:, :].T
    kt[:, width:] = k_ref[...].T
    vt[:, width:] = v_ref[...].T
    dk = dv = None
    for h in range(heads):
        hs = slice(h * hd, (h + 1) * hd)
        q = q_ref[h]
        do = do_ref[h]
        s = dot(k_ref[...], q, NT) * scale + bias[width:, :]
        p = jnp.exp2(s - st_ref[h, 0:1, :])
        ds = p * (dot(v_ref[...], do, NT) - st_ref[h, 1:2, :])
        p = p.astype(BF16)
        ds = ds.astype(BF16)
        o = dot(vt[:, :width], p_ref[h], NN) + dot(vt[:, width:], p, NN)
        out_ref[:, hs] = o.T.astype(BF16)
        g = dot(kt[:, :width], ds_ref[h], NN) + dot(kt[:, width:], ds, NN)
        dq_ref[:, hs] = (g * factor).T.astype(BF16)
        x = dot(ds, q, NN)
        y = dot(p, do, NN)
        dk = x if h == 0 else dk + x
        dv = y if h == 0 else dv + y
    mine_ref[0:rows, :] = dk * factor
    mine_ref[rows:, :] = dv


def call(kernel, name, outs, scratch, vmem, flops, *args):
    vm = pl.BlockSpec(memory_space=pltpu.VMEM)
    moved = sum(math.prod(a.shape) * a.dtype.itemsize for a in args)
    return pl.pallas_call(
        kernel,
        out_shape=[jax.ShapeDtypeStruct(*o) for o in outs],
        in_specs=[vm] * len(args),
        out_specs=[vm] * len(outs),
        scratch_shapes=[pltpu.VMEM(*s) for s in scratch],
        compiler_params=pltpu.CompilerParams(vmem_limit_bytes=vmem << 20),
        cost_estimate=pl.CostEstimate(flops=flops, bytes_accessed=moved, transcendentals=0),
        name=name,
    )(*args)


def attention_grads(lens, q, do, k, v, far, first_of):
    rows, hd = k.shape
    heads = q.shape[1] // hd
    width = REACH * rows
    block = 2 * heads * rows * rows * hd
    qs, dos, bias, st = call(
        functools.partial(local_kernel, first_of=first_of),
        "local",
        [((heads, rows, hd), BF16)] * 2 + [((width + rows, rows), F32), ((heads, 3, rows), F32)],
        [], 16, 2 * block, lens.reshape(1, -1), q, do, k, v,
    )
    *back, p, ds, st2 = call(
        remote_kernel,
        "remote",
        [((2 * rows, hd), BF16)] * REACH + [((heads, width, rows), BF16)] * 2 + [((heads, 2, rows), F32)],
        [((width, hd), BF16)] * 2
        + [((width, rows), F32)] * 2
        + [((8, rows), F32)]
        + [((width, hd), F32)] * 2,
        24, 16 * block, qs, dos, bias, st, *far,
    )
    return back, lambda: call(
        own_kernel,
        "own",
        [(q.shape, BF16)] * 2 + [((2 * rows, hd), F32)],
        [((hd, width + rows), BF16)] * 2,
        24, 14 * block, qs, dos, bias, st2, p, ds, k, v, *far,
    )


def shifted(block, distance):
    count = lax.axis_size("ctx") * lax.axis_size("grp")
    route = [(i, (i + distance) % count) for i in range(count)]
    return lax.ppermute(block, ("ctx", "grp"), route)


def body(queries, key_rows, value_rows, out_grad, doc_lengths):
    rows, hd = key_rows.shape

    def first_of():
        return (lax.axis_index("ctx") * lax.axis_size("grp") + lax.axis_index("grp")) * rows

    packed = jnp.concatenate([key_rows, value_rows], axis=0)
    far = [shifted(packed, d) for d in range(REACH, 0, -1)]
    back, finish = attention_grads(
        doc_lengths, queries, out_grad, key_rows, value_rows, far, first_of
    )
    came = [shifted(back[REACH - d], -d) for d in range(REACH, 0, -1)]
    attended, query_grad, total = finish()
    for part in came:
        total = total + part.astype(F32)
    total = total.astype(BF16)
    return attended, query_grad, total[:rows], total[rows:]


def solution(mesh):
    split = P(("ctx", "grp"), None)
    return jax.shard_map(
        body, mesh=mesh, in_specs=(split,) * 4 + (P(),), out_specs=(split,) * 4, check_vma=False
    )
```

```python
import functools
import math

import jax
import jax.numpy as jnp
from jax import lax
from jax.experimental import pallas as pl
from jax.experimental.pallas import tpu as pltpu
from jax.sharding import PartitionSpec as P

F32, BF16 = jnp.float32, jnp.bfloat16
NT = (((1,), (1,)), ((), ()))
NN = (((1,), (0,)), ((), ()))
LOG2E = 1.4426950408889634
REACH = 4
CHUNK = 64
STAGE_MB = 16


def dot(a, b, dims):
    return lax.dot_general(a, b, dims, preferred_element_type=F32)


def fold(x, op):
    return op(x.reshape(x.shape[0] // 8, 8, x.shape[1]), axis=0)


def stage_kernel(k_hbm, v_hbm, q_hbm, do_hbm, lens_hbm, packed, q, do, lens, sem):
    rows = k_hbm.shape[0]
    pairs = (
        (k_hbm, packed.at[0:rows, :]),
        (v_hbm, packed.at[rows : 2 * rows, :]),
        (q_hbm, q),
        (do_hbm, do),
        (lens_hbm, lens),
    )
    copies = [pltpu.make_async_copy(a, b, sem.at[i]) for i, (a, b) in enumerate(pairs)]
    for c in copies:
        c.start()
    for c in copies:
        c.wait()


def local_kernel(lens_ref, q_ref, do_ref, kv_ref, qs, dos, bias, st_ref, *, first_of):
    heads, rows, hd = qs.shape
    scale = LOG2E / math.sqrt(hd)
    q0 = first_of()
    nd = lens_ref.shape[1]
    lens = lens_ref[...]
    di = lax.broadcasted_iota(jnp.int32, (nd, nd), 0)
    dj = lax.broadcasted_iota(jnp.int32, (nd, nd), 1)
    ends = jnp.sum(jnp.where(dj <= di, lens, 0), axis=1, keepdims=True)
    length = jnp.sum(jnp.where(dj == di, lens, 0), axis=1, keepdims=True)
    qpos = q0 + lax.broadcasted_iota(jnp.int32, (1, rows), 1)
    begin = jnp.sum(jnp.where(ends <= qpos, length, 0), axis=0, keepdims=True)
    for b in range(REACH + 1):
        kpos = q0 + (b - REACH) * rows + lax.broadcasted_iota(jnp.int32, (rows, 1), 0)
        bias[b * rows : (b + 1) * rows, :] = jnp.where(
            (kpos >= begin) & (kpos <= qpos), 0.0, -jnp.inf
        )
    for h in range(heads):
        q = q_ref[:, h * hd : (h + 1) * hd]
        do = do_ref[:, h * hd : (h + 1) * hd]
        qs[h] = q
        dos[h] = do
        s = dot(kv_ref[0:rows, :], q, NT) * scale + bias[REACH * rows :, :]
        m = jnp.max(fold(s, jnp.max), axis=0, keepdims=True)
        p = jnp.exp2(s - m)
        dp = dot(kv_ref[rows:, :], do, NT)
        st_ref[h, 0:1, :] = m
        st_ref[h, 1:2, :] = jnp.sum(fold(p, jnp.sum), axis=0, keepdims=True)
        st_ref[h, 2:3, :] = jnp.sum(fold(p * dp, jnp.sum), axis=0, keepdims=True)


def remote_kernel(q_ref, do_ref, bias, st_ref, *refs):
    far = refs[:REACH]
    back = refs[REACH : 2 * REACH]
    p_out, ds_out, st_out, kall, vall, s_buf, dp_buf, m_buf, dv_acc, dk_acc = refs[2 * REACH :]
    heads, rows, hd = q_ref.shape
    width = REACH * rows
    factor = 1.0 / math.sqrt(hd)
    scale = factor * LOG2E
    for b in range(REACH):
        kall[b * rows : (b + 1) * rows, :] = far[b][0:rows, :]
        vall[b * rows : (b + 1) * rows, :] = far[b][rows:, :]
    chunks = [slice(c, c + CHUNK) for c in range(0, width, CHUNK)]

    def scores(h):
        s = dot(kall[...], q_ref[h], NT)
        dp = dot(vall[...], do_ref[h], NT)
        m = jnp.full((8, rows), -jnp.inf, F32)
        for cs in chunks:
            x = s[cs, :] * scale + bias[cs, :]
            m = jnp.maximum(m, fold(x, jnp.max))
            s_buf[cs, :] = x
            dp_buf[cs, :] = dp[cs, :]
        m_buf[...] = m

    def statistics(h):
        m0 = st_ref[h, 0:1, :]
        m = jnp.maximum(m0, jnp.max(m_buf[...], axis=0, keepdims=True))
        w0 = jnp.exp2(m0 - m)
        l = jnp.zeros((8, rows), F32)
        t = jnp.zeros((8, rows), F32)
        for cs in chunks:
            p = jnp.exp2(s_buf[cs, :] - m)
            l = l + fold(p, jnp.sum)
            t = t + fold(p * dp_buf[cs, :], jnp.sum)
        total = jnp.sum(l, axis=0, keepdims=True) + w0 * st_ref[h, 1:2, :]
        delta = (jnp.sum(t, axis=0, keepdims=True) + w0 * st_ref[h, 2:3, :]) / total
        lse = m + jnp.log2(total)
        st_out[h, 0:1, :] = lse
        st_out[h, 1:2, :] = delta
        return lse, delta

    def weights(h, lse, delta):
        for cs in chunks:
            p = jnp.exp2(s_buf[cs, :] - lse)
            p_out[h, cs, :] = p.astype(BF16)
            ds_out[h, cs, :] = (p * (dp_buf[cs, :] - delta)).astype(BF16)

    def grads(h):
        dv_acc[...] += dot(p_out[h], do_ref[h], NN)
        dk_acc[...] += dot(ds_out[h], q_ref[h], NN)

    dv_acc[...] = jnp.zeros_like(dv_acc)
    dk_acc[...] = jnp.zeros_like(dk_acc)
    scores(0)
    weights(0, *statistics(0))
    scores(1)

    @pl.loop(1, heads - 1)
    def _(h):
        grads(h - 1)
        weights(h, *statistics(h))
        scores(h + 1)

    grads(heads - 2)
    weights(heads - 1, *statistics(heads - 1))
    grads(heads - 1)
    for b in range(REACH):
        bs = slice(b * rows, (b + 1) * rows)
        back[b][0:rows, :] = (dk_acc[bs, :] * factor).astype(BF16)
        back[b][rows:, :] = dv_acc[bs, :].astype(BF16)


def own_kernel(q_ref, do_ref, bias, st_ref, p_ref, ds_ref, kv_ref, *refs):
    far = refs[:REACH]
    out_ref, dq_ref, mine_ref, kt, vt = refs[REACH:]
    heads, rows, hd = q_ref.shape
    width = REACH * rows
    factor = 1.0 / math.sqrt(hd)
    scale = factor * LOG2E
    for b in range(REACH):
        kt[:, b * rows : (b + 1) * rows] = far[b][0:rows, :].T
        vt[:, b * rows : (b + 1) * rows] = far[b][rows:, :].T
    k = kv_ref[0:rows, :]
    v = kv_ref[rows:, :]
    kt[:, width:] = k.T
    vt[:, width:] = v.T
    dk = dv = None
    for h in range(heads):
        hs = slice(h * hd, (h + 1) * hd)
        q = q_ref[h]
        do = do_ref[h]
        s = dot(k, q, NT) * scale + bias[width:, :]
        p = jnp.exp2(s - st_ref[h, 0:1, :])
        ds = p * (dot(v, do, NT) - st_ref[h, 1:2, :])
        p = p.astype(BF16)
        ds = ds.astype(BF16)
        o = dot(vt[:, :width], p_ref[h], NN) + dot(vt[:, width:], p, NN)
        out_ref[:, hs] = o.T.astype(BF16)
        g = dot(kt[:, :width], ds_ref[h], NN) + dot(kt[:, width:], ds, NN)
        dq_ref[:, hs] = (g * factor).T.astype(BF16)
        x = dot(ds, q, NN)
        y = dot(p, do, NN)
        dk = x if h == 0 else dk + x
        dv = y if h == 0 else dv + y
    mine_ref[0:rows, :] = dk * factor
    mine_ref[rows:, :] = dv


def call(kernel, name, outs, scratch, vmem, flops, *args, in_hbm=0):
    vm = pl.BlockSpec(memory_space=pltpu.VMEM)
    hbm = pl.BlockSpec(memory_space=pltpu.HBM)
    moved = sum(math.prod(a.shape) * a.dtype.itemsize for a in args)
    return pl.pallas_call(
        kernel,
        out_shape=[jax.ShapeDtypeStruct(*o) for o in outs],
        in_specs=[hbm] * in_hbm + [vm] * (len(args) - in_hbm),
        out_specs=[vm] * len(outs),
        scratch_shapes=[pltpu.VMEM(*s) if isinstance(s, tuple) else s for s in scratch],
        compiler_params=pltpu.CompilerParams(vmem_limit_bytes=int(vmem * 2**20)),
        cost_estimate=pl.CostEstimate(flops=flops, bytes_accessed=moved, transcendentals=0),
        name=name,
    )(*(pltpu.with_memory_space_constraint(a, pltpu.HBM) for a in args[:in_hbm]), *args[in_hbm:])


def stage(k, v, q, do, lens):
    rows, hd = k.shape
    return call(
        stage_kernel,
        "stage",
        [((2 * rows, hd), BF16), (q.shape, BF16), (do.shape, BF16), ((1, lens.shape[0]), jnp.int32)],
        [pltpu.SemaphoreType.DMA((5,))], STAGE_MB, 0, k, v, q, do, lens.reshape(1, -1), in_hbm=5,
    )


def attention_grads(lens, q, do, packed, far, first_of):
    rows, hd = packed.shape[0] // 2, packed.shape[1]
    heads = q.shape[1] // hd
    width = REACH * rows
    block = 2 * heads * rows * rows * hd
    qs, dos, bias, st = call(
        functools.partial(local_kernel, first_of=first_of),
        "local",
        [((heads, rows, hd), BF16)] * 2 + [((width + rows, rows), F32), ((heads, 3, rows), F32)],
        [], 16, 2 * block, lens, q, do, packed,
    )
    *back, p, ds, st2 = call(
        remote_kernel,
        "remote",
        [((2 * rows, hd), BF16)] * REACH + [((heads, width, rows), BF16)] * 2 + [((heads, 2, rows), F32)],
        [((width, hd), BF16)] * 2
        + [((width, rows), F32)] * 2
        + [((8, rows), F32)]
        + [((width, hd), F32)] * 2,
        24, 16 * block, qs, dos, bias, st, *far,
    )
    return back, lambda: call(
        own_kernel,
        "own",
        [(q.shape, BF16)] * 2 + [((2 * rows, hd), F32)],
        [((hd, width + rows), BF16)] * 2,
        24, 14 * block, qs, dos, bias, st2, p, ds, packed, *far,
    )


def shifted(block, distance):
    count = lax.axis_size("ctx") * lax.axis_size("grp")
    route = [(i, (i + distance) % count) for i in range(count)]
    return lax.ppermute(block, ("ctx", "grp"), route)


def body(queries, key_rows, value_rows, out_grad, doc_lengths):
    rows, hd = key_rows.shape

    def first_of():
        return (lax.axis_index("ctx") * lax.axis_size("grp") + lax.axis_index("grp")) * rows

    packed, q, do, lens = stage(key_rows, value_rows, queries, out_grad, doc_lengths)
    far = [shifted(packed, d) for d in range(REACH, 0, -1)]
    back, finish = attention_grads(
        lens, q, do, packed, far, first_of
    )
    came = [shifted(back[REACH - d], -d) for d in range(REACH, 0, -1)]
    attended, query_grad, total = finish()
    for part in came:
        total = total + part.astype(F32)
    total = total.astype(BF16)
    return attended, query_grad, total[:rows], total[rows:]


def solution(mesh):
    split = P(("ctx", "grp"), None)
    return jax.shard_map(
        body, mesh=mesh, in_specs=(split,) * 4 + (P(),), out_specs=(split,) * 4, check_vma=False
    )
```

```python
import functools
import math

import jax
import jax.numpy as jnp
from jax import lax
from jax.experimental import pallas as pl
from jax.experimental.pallas import tpu as pltpu
from jax.sharding import PartitionSpec as P

F32, BF16 = jnp.float32, jnp.bfloat16
NT = (((1,), (1,)), ((), ()))
NN = (((1,), (0,)), ((), ()))
LOG2E = 1.4426950408889634
REACH = 4
CHUNK = 64
STAGE_MB = 16


def dot(a, b, dims):
    return lax.dot_general(a, b, dims, preferred_element_type=F32)


def fold(x, op):
    return op(x.reshape(x.shape[0] // 8, 8, x.shape[1]), axis=0)


def stage_kernel(k_hbm, v_hbm, packed, sem):
    rows = k_hbm.shape[0]
    copies = [
        pltpu.make_async_copy(k_hbm, packed.at[0:rows, :], sem.at[0]),
        pltpu.make_async_copy(v_hbm, packed.at[rows : 2 * rows, :], sem.at[1]),
    ]
    for c in copies:
        c.start()
    for c in copies:
        c.wait()


def local_kernel(
    lens_hbm, q_hbm, do_hbm, kv_ref, qs, dos, dot_t, reach_ref, s_own, dp_own, m_own, l_own, o_own,
    lens_ref, q_ref, do_ref, sem, *, first_of
):
    heads, rows, hd = qs.shape
    scale = LOG2E / math.sqrt(hd)
    copies = [
        pltpu.make_async_copy(src, dst, sem.at[i])
        for i, (src, dst) in enumerate(((lens_hbm, lens_ref), (q_hbm, q_ref), (do_hbm, do_ref)))
    ]
    for c in copies:
        c.start()
    copies[0].wait()
    q0 = first_of()
    nd = lens_ref.shape[1]
    lens = lens_ref[...]
    di = lax.broadcasted_iota(jnp.int32, (nd, nd), 0)
    dj = lax.broadcasted_iota(jnp.int32, (nd, nd), 1)
    ends = jnp.sum(jnp.where(dj <= di, lens, 0), axis=1, keepdims=True)
    length = jnp.sum(jnp.where(dj == di, lens, 0), axis=1, keepdims=True)
    qpos = lax.broadcasted_iota(jnp.int32, (1, rows), 1)
    begin = jnp.sum(jnp.where(ends <= qpos + q0, length, 0), axis=0, keepdims=True) - q0
    reach_ref[...] = begin
    kpos = lax.broadcasted_iota(jnp.int32, (rows, 1), 0)
    hide = jnp.where((kpos >= begin) & (kpos <= qpos), 0.0, -jnp.inf)
    vt = kv_ref[rows:, :].T
    copies[1].wait()
    copies[2].wait()
    for h in range(heads):
        q = q_ref[:, h * hd : (h + 1) * hd]
        do = do_ref[:, h * hd : (h + 1) * hd]
        qs[h] = q
        dos[h] = do
        dot_t[h] = do.T
        s = dot(kv_ref[0:rows, :], q, NT) * scale + hide
        m = jnp.max(fold(s, jnp.max), axis=0, keepdims=True)
        p = jnp.exp2(s - m)
        s_own[h] = s
        dp_own[h] = dot(kv_ref[rows:, :], do, NT).astype(BF16)
        m_own[h] = m
        l_own[h] = jnp.sum(fold(p, jnp.sum), axis=0, keepdims=True)
        o_own[h] = dot(vt, p.astype(BF16), NN)


def score_kernel(q_ref, do_ref, begin_ref, kv_ref, s_out, dp_out, m_out, kt_out, vt_out, *, distance):
    heads, rows, hd = q_ref.shape
    scale = LOG2E / math.sqrt(hd)
    kpos = lax.broadcasted_iota(jnp.int32, (rows, 1), 0) - distance * rows
    hide = jnp.where(kpos >= begin_ref[...], 0.0, -jnp.inf)
    k = kv_ref[0:rows, :]
    v = kv_ref[rows:, :]
    for h in range(heads):
        s = dot(k, q_ref[h], NT) * scale + hide
        s_out[h] = s
        m_out[h] = fold(s, jnp.max)
        dp_out[h] = dot(v, do_ref[h], NT).astype(BF16)
    kt_out[...] = k.T
    vt_out[0:hd, :] = v.T
    vt_out[hd:, :] = jnp.ones((vt_out.shape[0] - hd, rows), BF16)


def remote_kernel(q_ref, do_ref, dot_t, m_own, l_own, o_own, *refs):
    parts = [refs[i * REACH : (i + 1) * REACH] for i in range(5)]
    s_in, dp_in, m_in, vt, back = parts
    ds_out, o_out, st_out, q_low, do_low, p_buf = refs[5 * REACH :]
    heads, rows, hd = q_ref.shape
    factor = 1.0 / math.sqrt(hd)
    blocks = [slice(b * rows, (b + 1) * rows) for b in range(REACH)]
    tiles = [(b, slice(c, c + CHUNK)) for b in range(REACH) for c in range(0, rows, CHUNK)]
    def weights(h):
        top = m_in[0][h]
        for b in range(1, REACH):
            top = jnp.maximum(top, m_in[b][h])
        m = jnp.maximum(m_own[h], jnp.max(top, axis=0, keepdims=True))
        st_out[h, 0:1, :] = m
        for b, cs in tiles:
            at = slice(b * rows + cs.start, b * rows + cs.stop)
            p_buf[h, at, :] = jnp.exp2(s_in[b][h, cs, :] - m).astype(BF16)

    def output(h):
        w = jnp.exp2(m_own[h] - st_out[h, 0:1, :])
        o = dot(vt[0][...], p_buf[h, blocks[0], :], NN)
        for b in range(1, REACH):
            o = o + dot(vt[b][...], p_buf[h, blocks[b], :], NN)
        inv = 1.0 / (o[hd : hd + 1, :] + w * l_own[h])
        o = (o[0:hd, :] + w * o_own[h]) * inv
        o_out[h] = o
        st_out[h, 1:2, :] = inv
        st_out[h, 2:3, :] = jnp.sum(fold(o * dot_t[h].astype(F32), jnp.sum), axis=0, keepdims=True)

    def scaled(h):
        col = jnp.broadcast_to(st_out[h, 1:2, :], (8, rows)).T[:, 0:1]
        q_low[h] = (q_ref[h].astype(F32) * col).astype(BF16)
        do_low[h] = (do_ref[h].astype(F32) * col).astype(BF16)

    def slopes(h):
        low = st_out[h, 2:3, :].astype(BF16)
        for b, cs in tiles:
            at = slice(b * rows + cs.start, b * rows + cs.stop)
            ds_out[h, at, :] = p_buf[h, at, :] * (dp_in[b][h, cs, :] - low)

    def each(first, count, *stages):
        @pl.loop(first, first + count)
        def _(h):
            for i, stage in enumerate(stages):
                stage(h - i)

    each(0, heads, weights)
    for h in range(heads):
        output(h)
    for h in range(heads):
        scaled(h); slopes(h)
    dk = dv = None
    for h in range(heads):
        x = dot(ds_out[h], q_low[h], NN)
        y = dot(p_buf[h], do_low[h], NN)
        dk = x if h == 0 else dk + x
        dv = y if h == 0 else dv + y
    for b, bs in enumerate(blocks):
        back[b][0:rows, :] = (dk[bs, :] * factor).astype(BF16)
        back[b][rows:, :] = dv[bs, :].astype(BF16)


def own_kernel(q_low, do_low, s_own, dp_own, st_ref, o_ref, ds_ref, kv_ref, *refs):
    kt = refs[:REACH]
    out_ref, dq_ref, mine_ref = refs[REACH:]
    heads, hd, rows = o_ref.shape
    factor = 1.0 / math.sqrt(hd)
    own_t = kv_ref[0:rows, :].T
    dk = dv = None
    for h in range(heads):
        hs = slice(h * hd, (h + 1) * hd)
        p = jnp.exp2(s_own[h] - st_ref[h, 0:1, :]).astype(BF16)
        ds = p * (dp_own[h] - st_ref[h, 2:3, :].astype(BF16))
        out_ref[:, hs] = o_ref[h].T.astype(BF16)
        g = dot(own_t, ds, NN)
        for b in range(REACH):
            g = g + dot(kt[b][...], ds_ref[h, b * rows : (b + 1) * rows, :], NN)
        dq_ref[:, hs] = (g * (st_ref[h, 1:2, :] * factor)).T.astype(BF16)
        x = dot(ds, q_low[h], NN)
        y = dot(p, do_low[h], NN)
        dk = x if h == 0 else dk + x
        dv = y if h == 0 else dv + y
    mine_ref[0:rows, :] = dk * factor
    mine_ref[rows:, :] = dv


def call(kernel, name, outs, scratch, vmem, flops, *args, in_hbm=0):
    vm = pl.BlockSpec(memory_space=pltpu.VMEM)
    hbm = pl.BlockSpec(memory_space=pltpu.HBM)
    moved = sum(math.prod(a.shape) * a.dtype.itemsize for a in args)
    return pl.pallas_call(
        kernel,
        out_shape=[jax.ShapeDtypeStruct(*o) for o in outs],
        in_specs=[hbm] * in_hbm + [vm] * (len(args) - in_hbm),
        out_specs=[vm] * len(outs),
        scratch_shapes=[pltpu.VMEM(*s) if isinstance(s, tuple) else s for s in scratch],
        compiler_params=pltpu.CompilerParams(vmem_limit_bytes=int(vmem * 2**20)),
        cost_estimate=pl.CostEstimate(flops=flops, bytes_accessed=moved, transcendentals=0),
        name=name,
    )(*(pltpu.with_memory_space_constraint(a, pltpu.HBM) for a in args[:in_hbm]), *args[in_hbm:])


def stage(k, v):
    rows, hd = k.shape
    return call(
        stage_kernel, "stage", [((2 * rows, hd), BF16)], [pltpu.SemaphoreType.DMA((2,))],
        STAGE_MB, 0, k, v, in_hbm=2,
    )[0]


def attention_grads(lens, q, do, packed, far, first_of):
    rows, hd = packed.shape[0] // 2, packed.shape[1]
    heads = q.shape[1] // hd
    width = REACH * rows
    block = 2 * heads * rows * rows * hd
    stack = ((heads, rows, hd), BF16)
    tall = (heads, hd, rows)
    line = ((heads, 1, rows), F32)
    square = (heads, rows, rows)
    qs, dos, dot_t, begin, s_own, dp_own, m_own, l_own, o_own = call(
        functools.partial(local_kernel, first_of=first_of),
        "local",
        [stack, stack, (tall, BF16), ((1, rows), jnp.int32), (square, F32), (square, BF16), line, line, (tall, F32)],
        [((1, lens.shape[0]), jnp.int32), (q.shape, BF16), (do.shape, BF16), pltpu.SemaphoreType.DMA((3,))],
        16, 3 * block, lens.reshape(1, -1), q, do, packed, in_hbm=3,
    )
    scored = [
        call(
            functools.partial(score_kernel, distance=REACH - b),
            "score",
            [(square, F32), (square, BF16), ((heads, 8, rows), F32), ((hd, rows), BF16), ((hd + 8, rows), BF16)],
            [], 12, 2 * block, qs, dos, begin, far[b],
        )
        for b in range(REACH)
    ]
    s, dp, m, kt, vt = zip(*scored)
    *back, ds, o, st, q_low, do_low = call(
        remote_kernel,
        "remote",
        [((2 * rows, hd), BF16)] * REACH
        + [((heads, width, rows), BF16), (tall, F32), ((heads, 3, rows), F32), stack, stack],
        [((heads, width, rows), BF16)],
        16, 12 * block, qs, dos, dot_t, m_own, l_own, o_own, *s, *dp, *m, *vt,
    )
    return back, lambda: call(
        own_kernel,
        "own",
        [(q.shape, BF16)] * 2 + [((2 * rows, hd), F32)],
        [],
        12, 7 * block, q_low, do_low, s_own, dp_own, st, o, ds, packed, *kt,
    )


def shifted(block, distance):
    count = lax.axis_size("ctx") * lax.axis_size("grp")
    route = [(i, (i + distance) % count) for i in range(count)]
    return lax.ppermute(block, ("ctx", "grp"), route)


def body(queries, key_rows, value_rows, out_grad, doc_lengths):
    rows, hd = key_rows.shape

    def first_of():
        return (lax.axis_index("ctx") * lax.axis_size("grp") + lax.axis_index("grp")) * rows

    packed = stage(key_rows, value_rows)
    far = [shifted(packed, d) for d in range(REACH, 0, -1)]
    back, finish = attention_grads(
        doc_lengths, queries, out_grad, packed, far, first_of
    )
    came = [shifted(back[REACH - d], -d) for d in range(REACH, 0, -1)]
    attended, query_grad, total = finish()
    for part in came:
        total = total + part.astype(F32)
    total = total.astype(BF16)
    return attended, query_grad, total[:rows], total[rows:]


def solution(mesh):
    split = P(("ctx", "grp"), None)
    return jax.shard_map(
        body, mesh=mesh, in_specs=(split,) * 4 + (P(),), out_specs=(split,) * 4, check_vma=False
    )
```

```python
import functools
import math

import jax
import jax.numpy as jnp
from jax import lax
from jax.experimental import pallas as pl
from jax.experimental.pallas import tpu as pltpu
from jax.sharding import PartitionSpec as P

F32, BF16 = jnp.float32, jnp.bfloat16
NT = (((1,), (1,)), ((), ()))
NN = (((1,), (0,)), ((), ()))
LOG2E = 1.4426950408889634
REACH = 4
CHUNK = 64
STAGE_MB = 16


def dot(a, b, dims):
    return lax.dot_general(a, b, dims, preferred_element_type=F32)


def fold(x, op):
    return op(x.reshape(x.shape[0] // 8, 8, x.shape[1]), axis=0)


def stage_kernel(k_hbm, v_hbm, packed, sem):
    rows = k_hbm.shape[0]
    copies = [
        pltpu.make_async_copy(k_hbm, packed.at[0:rows, :], sem.at[0]),
        pltpu.make_async_copy(v_hbm, packed.at[rows : 2 * rows, :], sem.at[1]),
    ]
    for c in copies:
        c.start()
    for c in copies:
        c.wait()


def local_kernel(
    lens_hbm, q_hbm, do_hbm, kv_ref, qs, dos, dot_t, reach_ref, s_own, dp_own, m_own, l_own, o_own,
    lens_ref, q_ref, do_ref, sem, *, first_of
):
    heads, rows, hd = qs.shape
    scale = LOG2E / math.sqrt(hd)
    copies = [
        pltpu.make_async_copy(src, dst, sem.at[i])
        for i, (src, dst) in enumerate(((lens_hbm, lens_ref), (q_hbm, q_ref), (do_hbm, do_ref)))
    ]
    for c in copies:
        c.start()
    copies[0].wait()
    q0 = first_of()
    nd = lens_ref.shape[1]
    lens = lens_ref[...]
    di = lax.broadcasted_iota(jnp.int32, (nd, nd), 0)
    dj = lax.broadcasted_iota(jnp.int32, (nd, nd), 1)
    ends = jnp.sum(jnp.where(dj <= di, lens, 0), axis=1, keepdims=True)
    length = jnp.sum(jnp.where(dj == di, lens, 0), axis=1, keepdims=True)
    qpos = lax.broadcasted_iota(jnp.int32, (1, rows), 1)
    begin = jnp.sum(jnp.where(ends <= qpos + q0, length, 0), axis=0, keepdims=True) - q0
    reach_ref[...] = begin
    kpos = lax.broadcasted_iota(jnp.int32, (rows, 1), 0)
    hide = jnp.where((kpos >= begin) & (kpos <= qpos), 0.0, -jnp.inf)
    vt = kv_ref[rows:, :].T
    copies[1].wait()
    copies[2].wait()
    for h in range(heads):
        q = q_ref[:, h * hd : (h + 1) * hd]
        do = do_ref[:, h * hd : (h + 1) * hd]
        qs[h] = q
        dos[h] = do
        dot_t[h] = do.T
        s = dot(kv_ref[0:rows, :], q, NT) * scale + hide
        m = jnp.max(fold(s, jnp.max), axis=0, keepdims=True)
        p = jnp.exp2(s - m)
        s_own[h] = s
        dp_own[h] = dot(kv_ref[rows:, :], do, NT)
        m_own[h] = m
        l_own[h] = jnp.sum(fold(p, jnp.sum), axis=0, keepdims=True)
        o_own[h] = dot(vt, p.astype(BF16), NN)


def score_kernel(q_ref, do_ref, begin_ref, kv_ref, s_out, dp_out, m_out, kt_out, vt_out, *, distance):
    heads, rows, hd = q_ref.shape
    scale = LOG2E / math.sqrt(hd)
    kpos = lax.broadcasted_iota(jnp.int32, (rows, 1), 0) - distance * rows
    hide = jnp.where(kpos >= begin_ref[...], 0.0, -jnp.inf)
    k = kv_ref[0:rows, :]
    v = kv_ref[rows:, :]
    kt_out[...] = k.T
    vt_out[0:hd, :] = v.T
    vt_out[hd:, :] = jnp.ones((vt_out.shape[0] - hd, rows), BF16)

    @pl.when(jnp.min(begin_ref[...]) < (1 - distance) * rows)
    def _():
        for h in range(heads):
            s = dot(k, q_ref[h], NT) * scale + hide
            s_out[h] = s
            m_out[h] = fold(s, jnp.max)
            dp_out[h] = dot(v, do_ref[h], NT)


def far_blocks(count, q_ref, do_ref, dot_t, m_own, l_own, o_own, *refs):
    parts = [refs[i * REACH : (i + 1) * REACH] for i in range(5)]
    s_in, dp_in, m_in, vt, back = parts
    ds_out, o_out, st_out, q_low, do_low, p_buf = refs[5 * REACH :]
    heads, rows, hd = q_ref.shape
    factor = 1.0 / math.sqrt(hd)
    seen = range(REACH - count, REACH)
    tiles = [(b, slice(c, c + CHUNK)) for b in seen for c in range(0, rows, CHUNK)]
    def weights(h):
        m = m_own[h]
        for b in seen:
            m = jnp.maximum(m, jnp.max(m_in[b][h], axis=0, keepdims=True))
        st_out[h, 0:1, :] = m
        for b, cs in tiles:
            at = slice(b * rows + cs.start, b * rows + cs.stop)
            p_buf[h, at, :] = jnp.exp2(s_in[b][h, cs, :] - m).astype(BF16)

    def output(h):
        w = jnp.exp2(m_own[h] - st_out[h, 0:1, :])
        total = w * l_own[h]
        o = w * o_own[h]
        if count:
            far_o = sum(dot(vt[b][...], p_buf[h, b * rows : (b + 1) * rows, :], NN) for b in seen)
            total = total + far_o[hd : hd + 1, :]
            o = o + far_o[0:hd, :]
        inv = 1.0 / total
        o = o * inv
        o_out[h] = o
        st_out[h, 1:2, :] = inv
        st_out[h, 2:3, :] = jnp.sum(fold(o * dot_t[h].astype(F32), jnp.sum), axis=0, keepdims=True)

    def scaled(h):
        col = jnp.broadcast_to(st_out[h, 1:2, :], (8, rows)).T[:, 0:1]
        q_low[h] = (q_ref[h].astype(F32) * col).astype(BF16)
        do_low[h] = (do_ref[h].astype(F32) * col).astype(BF16)

    def slopes(h):
        delta = st_out[h, 2:3, :]
        for b, cs in tiles:
            at = slice(b * rows + cs.start, b * rows + cs.stop)
            ds_out[h, at, :] = p_buf[h, at, :] * (dp_in[b][h, cs, :] - delta).astype(BF16)

    for h in range(heads):
        weights(h)
    for h in range(heads):
        output(h)
    for h in range(heads):
        scaled(h); slopes(h)
    low = (REACH - count) * rows
    if low:
        ds_out[:, 0:low, :] = jnp.zeros((heads, low, rows), BF16)
    for b in range(REACH - count):
        back[b][...] = jnp.zeros(back[b].shape, BF16)
    if not count:
        return
    dk = dv = None
    for h in range(heads):
        x = dot(ds_out[h, low:, :], q_low[h], NN)
        y = dot(p_buf[h, low:, :], do_low[h], NN)
        dk = x if h == 0 else dk + x
        dv = y if h == 0 else dv + y
    for i, b in enumerate(seen):
        bs = slice(i * rows, (i + 1) * rows)
        back[b][0:rows, :] = (dk[bs, :] * factor).astype(BF16)
        back[b][rows:, :] = dv[bs, :].astype(BF16)


def remote_kernel(begin_ref, *refs):
    first = jnp.min(begin_ref[...])
    rows = begin_ref.shape[1]
    for count in range(REACH + 1):
        near = first < (1 - count) * rows if count else first >= 0
        far = first >= -count * rows if count < REACH else first < (1 - REACH) * rows

        @pl.when(near & far)
        def _(count=count):
            far_blocks(count, *refs)


def own_kernel(q_low, do_low, s_own, dp_own, st_ref, o_ref, ds_ref, kv_ref, *refs):
    kt = refs[:REACH]
    out_ref, dq_ref, mine_ref = refs[REACH:]
    heads, hd, rows = o_ref.shape
    factor = 1.0 / math.sqrt(hd)
    own_t = kv_ref[0:rows, :].T
    dk = dv = None
    for h in range(heads):
        hs = slice(h * hd, (h + 1) * hd)
        p = jnp.exp2(s_own[h] - st_ref[h, 0:1, :]).astype(BF16)
        ds = p * (dp_own[h] - st_ref[h, 2:3, :]).astype(BF16)
        out_ref[:, hs] = o_ref[h].T.astype(BF16)
        g = dot(own_t, ds, NN)
        for b in range(REACH):
            g = g + dot(kt[b][...], ds_ref[h, b * rows : (b + 1) * rows, :], NN)
        dq_ref[:, hs] = (g * (st_ref[h, 1:2, :] * factor)).T.astype(BF16)
        x = dot(ds, q_low[h], NN)
        y = dot(p, do_low[h], NN)
        dk = x if h == 0 else dk + x
        dv = y if h == 0 else dv + y
    mine_ref[0:rows, :] = dk * factor
    mine_ref[rows:, :] = dv


def call(kernel, name, outs, scratch, vmem, flops, *args, in_hbm=0):
    vm = pl.BlockSpec(memory_space=pltpu.VMEM)
    hbm = pl.BlockSpec(memory_space=pltpu.HBM)
    moved = sum(math.prod(a.shape) * a.dtype.itemsize for a in args)
    return pl.pallas_call(
        kernel,
        out_shape=[jax.ShapeDtypeStruct(*o) for o in outs],
        in_specs=[hbm] * in_hbm + [vm] * (len(args) - in_hbm),
        out_specs=[vm] * len(outs),
        scratch_shapes=[pltpu.VMEM(*s) if isinstance(s, tuple) else s for s in scratch],
        compiler_params=pltpu.CompilerParams(vmem_limit_bytes=int(vmem * 2**20)),
        cost_estimate=pl.CostEstimate(flops=flops, bytes_accessed=moved, transcendentals=0),
        name=name,
    )(*(pltpu.with_memory_space_constraint(a, pltpu.HBM) for a in args[:in_hbm]), *args[in_hbm:])


def stage(k, v):
    rows, hd = k.shape
    return call(
        stage_kernel, "stage", [((2 * rows, hd), BF16)], [pltpu.SemaphoreType.DMA((2,))],
        STAGE_MB, 0, k, v, in_hbm=2,
    )[0]


def attention_grads(lens, q, do, packed, far, first_of):
    rows, hd = packed.shape[0] // 2, packed.shape[1]
    heads = q.shape[1] // hd
    width = REACH * rows
    block = 2 * heads * rows * rows * hd
    stack = ((heads, rows, hd), BF16)
    tall = (heads, hd, rows)
    line = ((heads, 1, rows), F32)
    square = (heads, rows, rows)
    qs, dos, dot_t, begin, s_own, dp_own, m_own, l_own, o_own = call(
        functools.partial(local_kernel, first_of=first_of),
        "local",
        [stack, stack, (tall, BF16), ((1, rows), jnp.int32), (square, F32), (square, F32), line, line, (tall, F32)],
        [((1, lens.shape[0]), jnp.int32), (q.shape, BF16), (do.shape, BF16), pltpu.SemaphoreType.DMA((3,))],
        16, 3 * block, lens.reshape(1, -1), q, do, packed, in_hbm=3,
    )
    scored = [
        call(
            functools.partial(score_kernel, distance=REACH - b),
            "score",
            [(square, F32), (square, F32), ((heads, 8, rows), F32), ((hd, rows), BF16), ((hd + 8, rows), BF16)],
            [], 12, 2 * block, qs, dos, begin, far[b],
        )
        for b in range(REACH)
    ]
    s, dp, m, kt, vt = zip(*scored)
    *back, ds, o, st, q_low, do_low = call(
        remote_kernel,
        "remote",
        [((2 * rows, hd), BF16)] * REACH
        + [((heads, width, rows), BF16), (tall, F32), ((heads, 3, rows), F32), stack, stack],
        [((heads, width, rows), BF16)],
        16, 12 * block, begin, qs, dos, dot_t, m_own, l_own, o_own, *s, *dp, *m, *vt,
    )
    return back, lambda: call(
        own_kernel,
        "own",
        [(q.shape, BF16)] * 2 + [((2 * rows, hd), F32)],
        [],
        12, 7 * block, q_low, do_low, s_own, dp_own, st, o, ds, packed, *kt,
    )


def shifted(block, distance):
    count = lax.axis_size("ctx") * lax.axis_size("grp")
    route = [(i, (i + distance) % count) for i in range(count)]
    return lax.ppermute(block, ("ctx", "grp"), route)


def body(queries, key_rows, value_rows, out_grad, doc_lengths):
    rows, hd = key_rows.shape

    def first_of():
        return (lax.axis_index("ctx") * lax.axis_size("grp") + lax.axis_index("grp")) * rows

    packed = stage(key_rows, value_rows)
    far = [shifted(packed, d) for d in range(REACH, 0, -1)]
    back, finish = attention_grads(
        doc_lengths, queries, out_grad, packed, far, first_of
    )
    came = [shifted(back[REACH - d], -d) for d in range(REACH, 0, -1)]
    attended, query_grad, total = finish()
    for part in came:
        total = total + part.astype(F32)
    total = total.astype(BF16)
    return attended, query_grad, total[:rows], total[rows:]


def solution(mesh):
    split = P(("ctx", "grp"), None)
    return jax.shard_map(
        body, mesh=mesh, in_specs=(split,) * 4 + (P(),), out_specs=(split,) * 4, check_vma=False
    )
```

```python
import functools
import math

import jax
import jax.numpy as jnp
from jax import lax
from jax.experimental import pallas as pl
from jax.experimental.pallas import tpu as pltpu
from jax.sharding import PartitionSpec as P

F32, BF16 = jnp.float32, jnp.bfloat16
NT = (((1,), (1,)), ((), ()))
NN = (((1,), (0,)), ((), ()))
LOG2E = 1.4426950408889634
REACH = 4
CHUNK = 64
STAGE_MB = 16


def dot(a, b, dims):
    return lax.dot_general(a, b, dims, preferred_element_type=F32)


def fold(x, op):
    return op(x.reshape(x.shape[0] // 8, 8, x.shape[1]), axis=0)


def stage_kernel(k_hbm, v_hbm, packed, sem):
    rows = k_hbm.shape[0]
    copies = [
        pltpu.make_async_copy(k_hbm, packed.at[0:rows, :], sem.at[0]),
        pltpu.make_async_copy(v_hbm, packed.at[rows : 2 * rows, :], sem.at[1]),
    ]
    for c in copies:
        c.start()
    for c in copies:
        c.wait()


def local_kernel(
    lens_hbm, q_hbm, do_hbm, kv_ref, qs, dos, dot_t, reach_ref, s_own, dp_own, m_own, l_own, o_own,
    lens_ref, q_ref, do_ref, sem, *, first_of
):
    heads, rows, hd = qs.shape
    scale = LOG2E / math.sqrt(hd)
    copies = [
        pltpu.make_async_copy(src, dst, sem.at[i])
        for i, (src, dst) in enumerate(((lens_hbm, lens_ref), (q_hbm, q_ref), (do_hbm, do_ref)))
    ]
    for c in copies:
        c.start()
    copies[0].wait()
    q0 = first_of()
    nd = lens_ref.shape[1]
    lens = lens_ref[...]
    di = lax.broadcasted_iota(jnp.int32, (nd, nd), 0)
    dj = lax.broadcasted_iota(jnp.int32, (nd, nd), 1)
    ends = jnp.sum(jnp.where(dj <= di, lens, 0), axis=1, keepdims=True)
    length = jnp.sum(jnp.where(dj == di, lens, 0), axis=1, keepdims=True)
    qpos = lax.broadcasted_iota(jnp.int32, (1, rows), 1)
    begin = jnp.sum(jnp.where(ends <= qpos + q0, length, 0), axis=0, keepdims=True) - q0
    reach_ref[...] = begin
    kpos = lax.broadcasted_iota(jnp.int32, (rows, 1), 0)
    hide = jnp.where((kpos >= begin) & (kpos <= qpos), 0.0, -jnp.inf)
    vt = kv_ref[rows:, :].T
    copies[1].wait()
    copies[2].wait()
    for h in range(heads):
        q = q_ref[:, h * hd : (h + 1) * hd]
        do = do_ref[:, h * hd : (h + 1) * hd]
        qs[h] = q
        dos[h] = do
        dot_t[h] = do.T
        s = dot(kv_ref[0:rows, :], q, NT) * scale + hide
        m = jnp.max(fold(s, jnp.max), axis=0, keepdims=True)
        p = jnp.exp2(s - m)
        s_own[h] = s
        dp_own[h] = dot(kv_ref[rows:, :], do, NT)
        m_own[h] = m
        l_own[h] = jnp.sum(fold(p, jnp.sum), axis=0, keepdims=True)
        o_own[h] = dot(vt, p.astype(BF16), NN)


def score_kernel(q_ref, do_ref, begin_ref, kv_ref, s_out, dp_out, m_out, kt_out, vt_out, *, distance):
    heads, rows, hd = q_ref.shape
    scale = LOG2E / math.sqrt(hd)
    kpos = lax.broadcasted_iota(jnp.int32, (rows, 1), 0) - distance * rows
    hide = jnp.where(kpos >= begin_ref[...], 0.0, -jnp.inf)
    k = kv_ref[0:rows, :]
    v = kv_ref[rows:, :]
    kt_out[...] = k.T
    vt_out[0:hd, :] = v.T
    vt_out[hd:, :] = jnp.ones((vt_out.shape[0] - hd, rows), BF16)

    @pl.when(jnp.min(begin_ref[...]) < (1 - distance) * rows)
    def _():
        for h in range(heads):
            s = dot(k, q_ref[h], NT) * scale + hide
            s_out[h] = s
            m_out[h] = fold(s, jnp.max)
            dp_out[h] = dot(v, do_ref[h], NT)


def far_blocks(count, q_ref, do_ref, dot_t, m_own, l_own, o_own, *refs):
    parts = [refs[i * REACH : (i + 1) * REACH] for i in range(5)]
    s_in, dp_in, m_in, vt, back = parts
    ds_out, o_out, st_out, q_low, do_low, p_buf = refs[5 * REACH :]
    heads, rows, hd = q_ref.shape
    factor = 1.0 / math.sqrt(hd)
    seen = range(REACH - count, REACH)
    tiles = [(b, slice(c, c + CHUNK)) for b in seen for c in range(0, rows, CHUNK)]
    def weights(h):
        m = m_own[h]
        for b in seen:
            m = jnp.maximum(m, jnp.max(m_in[b][h], axis=0, keepdims=True))
        st_out[h, 0:1, :] = m
        for b, cs in tiles:
            at = slice(b * rows + cs.start, b * rows + cs.stop)
            p_buf[h, at, :] = jnp.exp2(s_in[b][h, cs, :] - m).astype(BF16)

    def output(h):
        w = jnp.exp2(m_own[h] - st_out[h, 0:1, :])
        total = w * l_own[h]
        o = w * o_own[h]
        if count:
            far_o = sum(dot(vt[b][...], p_buf[h, b * rows : (b + 1) * rows, :], NN) for b in seen)
            total = total + far_o[hd : hd + 1, :]
            o = o + far_o[0:hd, :]
        inv = 1.0 / total
        o = o * inv
        o_out[h] = o
        st_out[h, 1:2, :] = inv
        st_out[h, 2:3, :] = jnp.sum(fold(o * dot_t[h].astype(F32), jnp.sum), axis=0, keepdims=True)

    def scaled(h):
        col = jnp.broadcast_to(st_out[h, 1:2, :], (8, rows)).T[:, 0:1]
        q_low[h] = (q_ref[h].astype(F32) * col).astype(BF16)
        do_low[h] = (do_ref[h].astype(F32) * col).astype(BF16)

    def slopes(h):
        delta = st_out[h, 2:3, :]
        for b, cs in tiles:
            at = slice(b * rows + cs.start, b * rows + cs.stop)
            ds_out[h, at, :] = p_buf[h, at, :] * (dp_in[b][h, cs, :] - delta).astype(BF16)

    for h in range(heads):
        weights(h)
    for h in range(heads):
        output(h)
    for h in range(heads):
        scaled(h); slopes(h)
    low = (REACH - count) * rows
    if low:
        ds_out[:, 0:low, :] = jnp.zeros((heads, low, rows), BF16)
    for b in range(REACH - count):
        back[b][...] = jnp.zeros(back[b].shape, BF16)
    if not count:
        return
    dk = dv = None
    for h in range(heads):
        x = dot(ds_out[h, low:, :], q_low[h], NN)
        y = dot(p_buf[h, low:, :], do_low[h], NN)
        dk = x if h == 0 else dk + x
        dv = y if h == 0 else dv + y
    for i, b in enumerate(seen):
        bs = slice(i * rows, (i + 1) * rows)
        back[b][0:rows, :] = (dk[bs, :] * factor).astype(BF16)
        back[b][rows:, :] = dv[bs, :].astype(BF16)


def remote_kernel(begin_ref, *refs):
    first = jnp.min(begin_ref[...])
    rows = begin_ref.shape[1]
    for count in range(REACH + 1):
        near = first < (1 - count) * rows if count else first >= 0
        far = first >= -count * rows if count < REACH else first < (1 - REACH) * rows

        @pl.when(near & far)
        def _(count=count):
            far_blocks(count, *refs)


def own_kernel(q_low, do_low, s_own, dp_own, st_ref, o_ref, ds_ref, kv_ref, *refs):
    kt = refs[:REACH]
    out_ref, dq_ref, mine_ref = refs[REACH:]
    heads, hd, rows = o_ref.shape
    factor = 1.0 / math.sqrt(hd)
    own_t = kv_ref[0:rows, :].T
    dk = dv = None
    for h in range(heads):
        hs = slice(h * hd, (h + 1) * hd)
        p = jnp.exp2(s_own[h] - st_ref[h, 0:1, :]).astype(BF16)
        ds = p * (dp_own[h] - st_ref[h, 2:3, :]).astype(BF16)
        out_ref[:, hs] = o_ref[h].T.astype(BF16)
        g = dot(own_t, ds, NN)
        for b in range(REACH):
            g = g + dot(kt[b][...], ds_ref[h, b * rows : (b + 1) * rows, :], NN)
        dq_ref[:, hs] = (g * (st_ref[h, 1:2, :] * factor)).T.astype(BF16)
        x = dot(ds, q_low[h], NN)
        y = dot(p, do_low[h], NN)
        dk = x if h == 0 else dk + x
        dv = y if h == 0 else dv + y
    mine_ref[0:rows, :] = dk * factor
    mine_ref[rows:, :] = dv


def call(kernel, name, outs, scratch, vmem, flops, *args, in_hbm=0):
    vm = pl.BlockSpec(memory_space=pltpu.VMEM)
    hbm = pl.BlockSpec(memory_space=pltpu.HBM)
    moved = sum(math.prod(a.shape) * a.dtype.itemsize for a in args)
    return pl.pallas_call(
        kernel,
        out_shape=[jax.ShapeDtypeStruct(*o) for o in outs],
        in_specs=[hbm] * in_hbm + [vm] * (len(args) - in_hbm),
        out_specs=[vm] * len(outs),
        scratch_shapes=[pltpu.VMEM(*s) if isinstance(s, tuple) else s for s in scratch],
        compiler_params=pltpu.CompilerParams(vmem_limit_bytes=int(vmem * 2**20)),
        cost_estimate=pl.CostEstimate(flops=flops, bytes_accessed=moved, transcendentals=0),
        name=name,
    )(*(pltpu.with_memory_space_constraint(a, pltpu.HBM) for a in args[:in_hbm]), *args[in_hbm:])


def stage(k, v):
    rows, hd = k.shape
    return call(
        stage_kernel, "stage", [((2 * rows, hd), BF16)], [pltpu.SemaphoreType.DMA((2,))],
        STAGE_MB, 0, k, v, in_hbm=2,
    )[0]


def attention_grads(lens, q, do, packed, far, first_of):
    rows, hd = packed.shape[0] // 2, packed.shape[1]
    heads = q.shape[1] // hd
    width = REACH * rows
    block = 2 * heads * rows * rows * hd
    stack = ((heads, rows, hd), BF16)
    tall = (heads, hd, rows)
    line = ((heads, 1, rows), F32)
    square = (heads, rows, rows)
    qs, dos, dot_t, begin, s_own, dp_own, m_own, l_own, o_own = call(
        functools.partial(local_kernel, first_of=first_of),
        "local",
        [stack, stack, (tall, BF16), ((1, rows), jnp.int32), (square, F32), (square, F32), line, line, (tall, F32)],
        [((1, lens.shape[0]), jnp.int32), (q.shape, BF16), (do.shape, BF16), pltpu.SemaphoreType.DMA((3,))],
        16, 3 * block, lens.reshape(1, -1), q, do, packed, in_hbm=3,
    )
    scored = [
        call(
            functools.partial(score_kernel, distance=REACH - b),
            "score",
            [(square, F32), (square, F32), ((heads, 8, rows), F32), ((hd, rows), BF16), ((hd + 8, rows), BF16)],
            [], 12, 2 * block, qs, dos, begin, far[b],
        )
        for b in range(REACH)
    ]
    s, dp, m, kt, vt = zip(*scored)
    *back, ds, o, st, q_low, do_low = call(
        remote_kernel,
        "remote",
        [((2 * rows, hd), BF16)] * REACH
        + [((heads, width, rows), BF16), (tall, F32), ((heads, 3, rows), F32), stack, stack],
        [((heads, width, rows), BF16)],
        16, 12 * block, begin, qs, dos, dot_t, m_own, l_own, o_own, *s, *dp, *m, *vt,
    )
    return back, lambda: call(
        own_kernel,
        "own",
        [(q.shape, BF16)] * 2 + [((2 * rows, hd), F32)],
        [],
        12, 7 * block, q_low, do_low, s_own, dp_own, st, o, ds, packed, *kt,
    )


def shifted(block, distance):
    count = lax.axis_size("ctx") * lax.axis_size("grp")
    route = [(i, (i + distance) % count) for i in range(count)]
    return lax.ppermute(block, ("ctx", "grp"), route)


def body(queries, key_rows, value_rows, out_grad, doc_lengths):
    rows, hd = key_rows.shape

    def first_of():
        return (lax.axis_index("ctx") * lax.axis_size("grp") + lax.axis_index("grp")) * rows

    packed = stage(key_rows, value_rows)
    far = [shifted(packed, d) for d in range(REACH, 0, -1)]
    back, finish = attention_grads(
        doc_lengths, queries, out_grad, packed, far, first_of
    )
    came = [shifted(back[REACH - d], -d) for d in range(1, REACH + 1)]
    attended, query_grad, total = finish()
    for part in came:
        total = total + part.astype(F32)
    total = total.astype(BF16)
    return attended, query_grad, total[:rows], total[rows:]


def solution(mesh):
    split = P(("ctx", "grp"), None)
    return jax.shard_map(
        body, mesh=mesh, in_specs=(split,) * 4 + (P(),), out_specs=(split,) * 4, check_vma=False
    )
```

```python
import functools
import math

import jax
import jax.numpy as jnp
from jax import lax
from jax.experimental import pallas as pl
from jax.experimental.pallas import tpu as pltpu
from jax.sharding import PartitionSpec as P

F32, BF16 = jnp.float32, jnp.bfloat16
NT = (((1,), (1,)), ((), ()))
NN = (((1,), (0,)), ((), ()))
LOG2E = 1.4426950408889634
REACH = 4
CHUNK = 64
STAGE_MB = 16


def dot(a, b, dims):
    return lax.dot_general(a, b, dims, preferred_element_type=F32)


def fold(x, op):
    return op(x.reshape(x.shape[0] // 8, 8, x.shape[1]), axis=0)


def stage_kernel(k_hbm, v_hbm, packed, sem):
    rows = k_hbm.shape[0]
    copies = [
        pltpu.make_async_copy(k_hbm, packed.at[0:rows, :], sem.at[0]),
        pltpu.make_async_copy(v_hbm, packed.at[rows : 2 * rows, :], sem.at[1]),
    ]
    for c in copies:
        c.start()
    for c in copies:
        c.wait()


def local_kernel(
    lens_hbm, q_hbm, do_hbm, kv_ref, qs, dos, dot_t, reach_ref, s_own, dp_own, m_own, l_own, o_own,
    lens_ref, q_ref, do_ref, sem, *, first_of
):
    heads, rows, hd = qs.shape
    scale = LOG2E / math.sqrt(hd)
    copies = [
        pltpu.make_async_copy(src, dst, sem.at[i])
        for i, (src, dst) in enumerate(((lens_hbm, lens_ref), (q_hbm, q_ref), (do_hbm, do_ref)))
    ]
    for c in copies:
        c.start()
    copies[0].wait()
    q0 = first_of()
    nd = lens_ref.shape[1]
    lens = lens_ref[...]
    di = lax.broadcasted_iota(jnp.int32, (nd, nd), 0)
    dj = lax.broadcasted_iota(jnp.int32, (nd, nd), 1)
    ends = jnp.sum(jnp.where(dj <= di, lens, 0), axis=1, keepdims=True)
    length = jnp.sum(jnp.where(dj == di, lens, 0), axis=1, keepdims=True)
    qpos = lax.broadcasted_iota(jnp.int32, (1, rows), 1)
    begin = jnp.sum(jnp.where(ends <= qpos + q0, length, 0), axis=0, keepdims=True) - q0
    reach_ref[...] = begin
    kpos = lax.broadcasted_iota(jnp.int32, (rows, 1), 0)
    hide = jnp.where((kpos >= begin) & (kpos <= qpos), 0.0, -jnp.inf)
    vt = kv_ref[rows:, :].T
    copies[1].wait()
    copies[2].wait()
    for h in range(heads):
        q = q_ref[:, h * hd : (h + 1) * hd]
        do = do_ref[:, h * hd : (h + 1) * hd]
        qs[h] = q
        dos[h] = do
        dot_t[h] = do.T
        s = dot(kv_ref[0:rows, :], q, NT) * scale + hide
        m = jnp.max(fold(s, jnp.max), axis=0, keepdims=True)
        p = jnp.exp2(s - m)
        s_own[h] = s
        dp_own[h] = dot(kv_ref[rows:, :], do, NT)
        m_own[h] = m
        l_own[h] = jnp.sum(fold(p, jnp.sum), axis=0, keepdims=True)
        o_own[h] = dot(vt, p.astype(BF16), NN)


def score_block(q_ref, do_ref, begin, kv_ref, s_out, dp_out, m_out, distance):
    heads, rows, hd = q_ref.shape
    scale = LOG2E / math.sqrt(hd)
    kpos = lax.broadcasted_iota(jnp.int32, (rows, 1), 0) - distance * rows
    hide = jnp.where(kpos >= begin, 0.0, -jnp.inf)
    for h in range(heads):
        s = dot(kv_ref[0:rows, :], q_ref[h], NT) * scale + hide
        s_out[h] = s
        m_out[h] = fold(s, jnp.max)
        dp_out[h] = dot(kv_ref[rows:, :], do_ref[h], NT)


def turned(kv_ref, kt_out, vt_out):
    rows, hd = kv_ref.shape[0] // 2, kv_ref.shape[1]
    kt_out[...] = kv_ref[0:rows, :].T
    vt_out[0:hd, :] = kv_ref[rows:, :].T
    vt_out[hd:, :] = jnp.ones((vt_out.shape[0] - hd, rows), BF16)


def score_kernel(q_ref, do_ref, begin_ref, kv_ref, s_out, dp_out, m_out, kt_out, vt_out, *, distance):
    rows = begin_ref.shape[1]
    turned(kv_ref, kt_out, vt_out)

    @pl.when(jnp.min(begin_ref[...]) < (1 - distance) * rows)
    def _():
        score_block(q_ref, do_ref, begin_ref[...], kv_ref, s_out, dp_out, m_out, distance)


def far_blocks(count, q_ref, do_ref, dot_t, m_own, l_own, o_own, *refs):
    s_in, dp_in, m_in, vt, back = [refs[i * REACH : (i + 1) * REACH] for i in range(5)]
    ds_out, o_out, st_out, q_low, do_low, p_buf = refs[5 * REACH :]
    heads, rows, hd = q_ref.shape
    factor = 1.0 / math.sqrt(hd)
    seen = range(REACH - count, REACH)
    tiles = [(b, slice(c, c + CHUNK)) for b in seen for c in range(0, rows, CHUNK)]
    def weights(h):
        m = m_own[h]
        for b in seen:
            m = jnp.maximum(m, jnp.max(m_in[b][h], axis=0, keepdims=True))
        st_out[h, 0:1, :] = m
        for b, cs in tiles:
            at = slice(b * rows + cs.start, b * rows + cs.stop)
            p_buf[h, at, :] = jnp.exp2(s_in[b][h, cs, :] - m).astype(BF16)

    def output(h):
        w = jnp.exp2(m_own[h] - st_out[h, 0:1, :])
        total = w * l_own[h]
        o = w * o_own[h]
        if count:
            far_o = sum(dot(vt[b][...], p_buf[h, b * rows : (b + 1) * rows, :], NN) for b in seen)
            total = total + far_o[hd : hd + 1, :]
            o = o + far_o[0:hd, :]
        inv = 1.0 / total
        o = o * inv
        o_out[h] = o
        st_out[h, 1:2, :] = inv
        st_out[h, 2:3, :] = jnp.sum(fold(o * dot_t[h].astype(F32), jnp.sum), axis=0, keepdims=True)

    def scaled(h):
        col = jnp.broadcast_to(st_out[h, 1:2, :], (8, rows)).T[:, 0:1]
        q_low[h] = (q_ref[h].astype(F32) * col).astype(BF16)
        do_low[h] = (do_ref[h].astype(F32) * col).astype(BF16)

    def slopes(h):
        delta = st_out[h, 2:3, :]
        for b, cs in tiles:
            at = slice(b * rows + cs.start, b * rows + cs.stop)
            ds_out[h, at, :] = p_buf[h, at, :] * (dp_in[b][h, cs, :] - delta).astype(BF16)

    low = (REACH - count) * rows
    for b in range(REACH - count):
        back[b][...] = jnp.zeros(back[b].shape, BF16)

    def prepare(hs):
        for h in hs:
            weights(h)
        for h in hs:
            output(h)
        for h in hs:
            scaled(h)
            slopes(h)

    def grads(hs):
        dk = dv = None
        for h in hs:
            x = dot(ds_out[h, low:, :], q_low[h], NN)
            y = dot(p_buf[h, low:, :], do_low[h], NN)
            dk = x if dk is None else dk + x
            dv = y if dv is None else dv + y
        return dk, dv

    group = 2
    sets = [range(g, g + group) for g in range(0, heads, group)]
    parts = []
    for g, hs in enumerate(sets):
        prepare(hs)
        if count and g:
            parts.append(grads(sets[g - 1]))
    if not count:
        return
    parts.append(grads(sets[-1]))
    dk = sum(p[0] for p in parts)
    dv = sum(p[1] for p in parts)
    for i, b in enumerate(seen):
        bs = slice(i * rows, (i + 1) * rows)
        back[b][0:rows, :] = (dk[bs, :] * factor).astype(BF16)
        back[b][rows:, :] = dv[bs, :].astype(BF16)


def by_count(begin_ref, run):
    first = jnp.min(begin_ref[...])
    rows = begin_ref.shape[1]
    for count in range(REACH + 1):
        near = first < (1 - count) * rows if count else first >= 0
        far = first >= -count * rows if count < REACH else first < (1 - REACH) * rows

        @pl.when(near & far)
        def _(count=count):
            run(count)


def remote_kernel(begin_ref, kv_ref, q_ref, do_ref, dot_t, m_own, l_own, o_own, *refs):
    near = REACH - 1
    s_in, dp_in, m_in, vt = [refs[i * near : (i + 1) * near] for i in range(4)]
    *outs, kt_out, p_buf, s_far, dp_far, m_far, vt_far = refs[4 * near :]

    def run(count):
        if count == REACH:
            turned(kv_ref, kt_out, vt_far)
            score_block(q_ref, do_ref, begin_ref[...], kv_ref, s_far, dp_far, m_far, REACH)
        far_blocks(
            count, q_ref, do_ref, dot_t, m_own, l_own, o_own,
            s_far, *s_in, dp_far, *dp_in, m_far, *m_in, vt_far, *vt, *outs, p_buf,
        )

    by_count(begin_ref, run)


def own_kernel(begin_ref, q_low, do_low, s_own, dp_own, st_ref, o_ref, ds_ref, kv_ref, *refs):
    kt = refs[:REACH]
    out_ref, dq_ref, mine_ref = refs[REACH:]
    heads, hd, rows = o_ref.shape
    factor = 1.0 / math.sqrt(hd)

    def run(count):
        own_t = kv_ref[0:rows, :].T
        dk = dv = None
        for h in range(heads):
            hs = slice(h * hd, (h + 1) * hd)
            p = jnp.exp2(s_own[h] - st_ref[h, 0:1, :]).astype(BF16)
            ds = p * (dp_own[h] - st_ref[h, 2:3, :]).astype(BF16)
            out_ref[:, hs] = o_ref[h].T.astype(BF16)
            g = dot(own_t, ds, NN)
            for b in range(REACH - count, REACH):
                g = g + dot(kt[b][...], ds_ref[h, b * rows : (b + 1) * rows, :], NN)
            dq_ref[:, hs] = (g * (st_ref[h, 1:2, :] * factor)).T.astype(BF16)
            x = dot(ds, q_low[h], NN)
            y = dot(p, do_low[h], NN)
            dk = x if h == 0 else dk + x
            dv = y if h == 0 else dv + y
        mine_ref[0:rows, :] = dk * factor
        mine_ref[rows:, :] = dv

    by_count(begin_ref, run)


def call(kernel, name, outs, scratch, vmem, flops, *args, in_hbm=0):
    vm = pl.BlockSpec(memory_space=pltpu.VMEM)
    hbm = pl.BlockSpec(memory_space=pltpu.HBM)
    moved = sum(math.prod(a.shape) * a.dtype.itemsize for a in args)
    return pl.pallas_call(
        kernel,
        out_shape=[jax.ShapeDtypeStruct(*o) for o in outs],
        in_specs=[hbm] * in_hbm + [vm] * (len(args) - in_hbm),
        out_specs=[vm] * len(outs),
        scratch_shapes=[pltpu.VMEM(*s) if isinstance(s, tuple) else s for s in scratch],
        compiler_params=pltpu.CompilerParams(vmem_limit_bytes=int(vmem * 2**20)),
        cost_estimate=pl.CostEstimate(flops=flops, bytes_accessed=moved, transcendentals=0),
        name=name,
    )(*(pltpu.with_memory_space_constraint(a, pltpu.HBM) for a in args[:in_hbm]), *args[in_hbm:])


def stage(k, v):
    rows, hd = k.shape
    return call(
        stage_kernel, "stage", [((2 * rows, hd), BF16)], [pltpu.SemaphoreType.DMA((2,))],
        STAGE_MB, 0, k, v, in_hbm=2,
    )[0]


def attention_grads(lens, q, do, packed, far, first_of):
    rows, hd = packed.shape[0] // 2, packed.shape[1]
    heads = q.shape[1] // hd
    width = REACH * rows
    block = 2 * heads * rows * rows * hd
    stack = ((heads, rows, hd), BF16)
    tall = (heads, hd, rows)
    line = ((heads, 1, rows), F32)
    square = (heads, rows, rows)
    qs, dos, dot_t, begin, s_own, dp_own, m_own, l_own, o_own = call(
        functools.partial(local_kernel, first_of=first_of),
        "local",
        [stack, stack, (tall, BF16), ((1, rows), jnp.int32), (square, F32), (square, F32), line, line, (tall, F32)],
        [((1, lens.shape[0]), jnp.int32), (q.shape, BF16), (do.shape, BF16), pltpu.SemaphoreType.DMA((3,))],
        16, 3 * block, lens.reshape(1, -1), q, do, packed, in_hbm=3,
    )
    scored = [
        call(
            functools.partial(score_kernel, distance=REACH - b),
            "score",
            [(square, F32), (square, F32), ((heads, 8, rows), F32), ((hd, rows), BF16), ((hd + 8, rows), BF16)],
            [], 12, 2 * block, qs, dos, begin, far[b],
        )
        for b in range(1, REACH)
    ]
    s, dp, m, kt, vt = zip(*scored)
    *back, ds, o, st, q_low, do_low, kt_far = call(
        remote_kernel,
        "remote",
        [((2 * rows, hd), BF16)] * REACH
        + [((heads, width, rows), BF16), (tall, F32), ((heads, 3, rows), F32), stack, stack, ((hd, rows), BF16)],
        [((heads, width, rows), BF16), (square, F32), (square, F32), ((heads, 8, rows), F32), ((hd + 8, rows), BF16)],
        24, 12 * block, begin, far[0], qs, dos, dot_t, m_own, l_own, o_own, *s, *dp, *m, *vt,
    )
    return back, lambda: call(
        own_kernel,
        "own",
        [(q.shape, BF16)] * 2 + [((2 * rows, hd), F32)],
        [],
        12, 7 * block, begin, q_low, do_low, s_own, dp_own, st, o, ds, packed, kt_far, *kt,
    )


def shifted(block, distance):
    count = lax.axis_size("ctx") * lax.axis_size("grp")
    route = [(i, (i + distance) % count) for i in range(count)]
    return lax.ppermute(block, ("ctx", "grp"), route)


def body(queries, key_rows, value_rows, out_grad, doc_lengths):
    rows, hd = key_rows.shape

    def first_of():
        return (lax.axis_index("ctx") * lax.axis_size("grp") + lax.axis_index("grp")) * rows

    packed = stage(key_rows, value_rows)
    far = [shifted(packed, d) for d in range(REACH, 0, -1)]
    back, finish = attention_grads(
        doc_lengths, queries, out_grad, packed, far, first_of
    )
    came = [shifted(back[REACH - d], -d) for d in range(1, REACH + 1)]
    attended, query_grad, total = finish()
    for part in came:
        total = total + part.astype(F32)
    total = total.astype(BF16)
    return attended, query_grad, total[:rows], total[rows:]


def solution(mesh):
    split = P(("ctx", "grp"), None)
    return jax.shard_map(
        body, mesh=mesh, in_specs=(split,) * 4 + (P(),), out_specs=(split,) * 4, check_vma=False
    )
```

```python
import functools
import math

import jax
import jax.numpy as jnp
from jax import lax
from jax.experimental import pallas as pl
from jax.experimental.pallas import tpu as pltpu
from jax.sharding import PartitionSpec as P

F32, BF16 = jnp.float32, jnp.bfloat16
NT = (((1,), (1,)), ((), ()))
NN = (((1,), (0,)), ((), ()))
LOG2E = 1.4426950408889634
REACH = 4
CHUNK = 64
STAGE_MB = 16


def dot(a, b, dims):
    return lax.dot_general(a, b, dims, preferred_element_type=F32)


def fold(x, op):
    return op(x.reshape(x.shape[0] // 8, 8, x.shape[1]), axis=0)


def stage_kernel(k_hbm, v_hbm, packed, sem):
    rows = k_hbm.shape[0]
    copies = [
        pltpu.make_async_copy(k_hbm, packed.at[0:rows, :], sem.at[0]),
        pltpu.make_async_copy(v_hbm, packed.at[rows : 2 * rows, :], sem.at[1]),
    ]
    for c in copies:
        c.start()
    for c in copies:
        c.wait()


def local_kernel(
    lens_hbm, q_hbm, do_hbm, kv_ref, qs, dos, dot_t, reach_ref, s_own, dp_own, m_own, l_own, o_own,
    lens_ref, q_ref, do_ref, sem, *, first_of
):
    heads, rows, hd = qs.shape
    scale = LOG2E / math.sqrt(hd)
    copies = [
        pltpu.make_async_copy(src, dst, sem.at[i])
        for i, (src, dst) in enumerate(((lens_hbm, lens_ref), (q_hbm, q_ref), (do_hbm, do_ref)))
    ]
    for c in copies:
        c.start()
    copies[0].wait()
    q0 = first_of()
    nd = lens_ref.shape[1]
    lens = lens_ref[...]
    di = lax.broadcasted_iota(jnp.int32, (nd, nd), 0)
    dj = lax.broadcasted_iota(jnp.int32, (nd, nd), 1)
    ends = jnp.sum(jnp.where(dj <= di, lens, 0), axis=1, keepdims=True)
    length = jnp.sum(jnp.where(dj == di, lens, 0), axis=1, keepdims=True)
    qpos = lax.broadcasted_iota(jnp.int32, (1, rows), 1)
    begin = jnp.sum(jnp.where(ends <= qpos + q0, length, 0), axis=0, keepdims=True) - q0
    reach_ref[...] = begin
    kpos = lax.broadcasted_iota(jnp.int32, (rows, 1), 0)
    hide = jnp.where((kpos >= begin) & (kpos <= qpos), 0.0, -jnp.inf)
    vt = kv_ref[rows:, :].T
    copies[1].wait()
    copies[2].wait()
    for h in range(heads):
        q = q_ref[:, h * hd : (h + 1) * hd]
        do = do_ref[:, h * hd : (h + 1) * hd]
        qs[h] = q
        dos[h] = do
        dot_t[h] = do.T
        s = dot(kv_ref[0:rows, :], q, NT) * scale + hide
        m = jnp.max(fold(s, jnp.max), axis=0, keepdims=True)
        p = jnp.exp2(s - m)
        s_own[h] = s
        dp_own[h] = dot(kv_ref[rows:, :], do, NT)
        m_own[h] = m
        l_own[h] = jnp.sum(fold(p, jnp.sum), axis=0, keepdims=True)
        o_own[h] = dot(vt, p.astype(BF16), NN)


def score_block(q_ref, do_ref, begin, kv_ref, s_out, dp_out, m_out, distance):
    heads, rows, hd = q_ref.shape
    scale = LOG2E / math.sqrt(hd)
    kpos = lax.broadcasted_iota(jnp.int32, (rows, 1), 0) - distance * rows
    hide = jnp.where(kpos >= begin, 0.0, -jnp.inf)
    for h in range(heads):
        s = dot(kv_ref[0:rows, :], q_ref[h], NT) * scale + hide
        s_out[h] = s
        m_out[h] = fold(s, jnp.max)
        dp_out[h] = dot(kv_ref[rows:, :], do_ref[h], NT)


def turned(kv_ref, kt_out, vt_out):
    rows, hd = kv_ref.shape[0] // 2, kv_ref.shape[1]
    kt_out[...] = kv_ref[0:rows, :].T
    vt_out[0:hd, :] = kv_ref[rows:, :].T
    vt_out[hd:, :] = jnp.ones((vt_out.shape[0] - hd, rows), BF16)


def score_kernel(q_ref, do_ref, begin_ref, kv_ref, s_out, dp_out, m_out, kt_out, vt_out, *, distance):
    rows = begin_ref.shape[1]
    turned(kv_ref, kt_out, vt_out)

    @pl.when(jnp.min(begin_ref[...]) < (1 - distance) * rows)
    def _():
        score_block(q_ref, do_ref, begin_ref[...], kv_ref, s_out, dp_out, m_out, distance)


def far_blocks(count, q_ref, do_ref, dot_t, m_own, l_own, o_own, *refs):
    s_in, dp_in, m_in, vt, back = [refs[i * REACH : (i + 1) * REACH] for i in range(5)]
    ds_out, o_out, st_out, q_low, do_low, p_buf = refs[5 * REACH :]
    heads, rows, hd = q_ref.shape
    factor = 1.0 / math.sqrt(hd)
    seen = range(REACH - count, REACH)
    tiles = [(b, slice(c, c + CHUNK)) for b in seen for c in range(0, rows, CHUNK)]
    def weights(h):
        m = m_own[h]
        for b in seen:
            m = jnp.maximum(m, jnp.max(m_in[b][h], axis=0, keepdims=True))
        st_out[h, 0:1, :] = m
        for b, cs in tiles:
            at = slice(b * rows + cs.start, b * rows + cs.stop)
            p_buf[h, at, :] = jnp.exp2(s_in[b][h, cs, :] - m).astype(BF16)

    def output(h):
        w = jnp.exp2(m_own[h] - st_out[h, 0:1, :])
        total = w * l_own[h]
        o = w * o_own[h]
        if count:
            far_o = sum(dot(vt[b][...], p_buf[h, b * rows : (b + 1) * rows, :], NN) for b in seen)
            total = total + far_o[hd : hd + 1, :]
            o = o + far_o[0:hd, :]
        inv = 1.0 / total
        o = o * inv
        o_out[h] = o
        st_out[h, 1:2, :] = inv
        st_out[h, 2:3, :] = jnp.sum(fold(o * dot_t[h].astype(F32), jnp.sum), axis=0, keepdims=True)

    def scaled(h):
        col = jnp.broadcast_to(st_out[h, 1:2, :], (8, rows)).T[:, 0:1]
        q_low[h] = (q_ref[h].astype(F32) * col).astype(BF16)
        do_low[h] = (do_ref[h].astype(F32) * col).astype(BF16)

    def slopes(h):
        delta = st_out[h, 2:3, :]
        for b, cs in tiles:
            at = slice(b * rows + cs.start, b * rows + cs.stop)
            ds_out[h, at, :] = p_buf[h, at, :] * (dp_in[b][h, cs, :] - delta).astype(BF16)

    low = (REACH - count) * rows
    for b in range(REACH - count):
        back[b][...] = jnp.zeros(back[b].shape, BF16)

    def prepare(hs):
        for h in hs:
            weights(h)
        for h in hs:
            output(h)
        for h in hs:
            scaled(h)
            slopes(h)

    def grads(hs):
        dk = dv = None
        for h in hs:
            x = dot(ds_out[h, low:, :], q_low[h], NN)
            y = dot(p_buf[h, low:, :], do_low[h], NN)
            dk = x if dk is None else dk + x
            dv = y if dv is None else dv + y
        return dk, dv

    group = 2
    sets = [range(g, g + group) for g in range(0, heads, group)]
    parts = []
    for g, hs in enumerate(sets):
        prepare(hs)
        if count and g:
            parts.append(grads(sets[g - 1]))
    if not count:
        return
    parts.append(grads(sets[-1]))
    dk = sum(p[0] for p in parts)
    dv = sum(p[1] for p in parts)
    for i, b in enumerate(seen):
        bs = slice(i * rows, (i + 1) * rows)
        back[b][0:rows, :] = (dk[bs, :] * factor).astype(BF16)
        back[b][rows:, :] = dv[bs, :].astype(BF16)


def by_count(begin_ref, run):
    first = jnp.min(begin_ref[...])
    rows = begin_ref.shape[1]
    for count in range(REACH + 1):
        near = first < (1 - count) * rows if count else first >= 0
        far = first >= -count * rows if count < REACH else first < (1 - REACH) * rows

        @pl.when(near & far)
        def _(count=count):
            run(count)


def remote_kernel(begin_ref, kv_ref, q_ref, do_ref, dot_t, m_own, l_own, o_own, *refs):
    near = REACH - 1
    s_in, dp_in, m_in, vt = [refs[i * near : (i + 1) * near] for i in range(4)]
    *outs, kt_out, p_buf, s_far, dp_far, m_far, vt_far = refs[4 * near :]

    def run(count):
        if count == REACH:
            turned(kv_ref, kt_out, vt_far)
            score_block(q_ref, do_ref, begin_ref[...], kv_ref, s_far, dp_far, m_far, REACH)
        far_blocks(
            count, q_ref, do_ref, dot_t, m_own, l_own, o_own,
            s_far, *s_in, dp_far, *dp_in, m_far, *m_in, vt_far, *vt, *outs, p_buf,
        )

    by_count(begin_ref, run)


def own_kernel(begin_ref, q_low, do_low, s_own, dp_own, st_ref, o_ref, ds_ref, kv_ref, *refs):
    kt = refs[:REACH]
    out_ref, dq_ref, mine_ref = refs[REACH:]
    heads, hd, rows = o_ref.shape
    factor = 1.0 / math.sqrt(hd)

    def run(count):
        own_t = kv_ref[0:rows, :].T
        dk = dv = None
        for h in range(heads):
            hs = slice(h * hd, (h + 1) * hd)
            p = jnp.exp2(s_own[h] - st_ref[h, 0:1, :]).astype(BF16)
            ds = p * (dp_own[h] - st_ref[h, 2:3, :]).astype(BF16)
            out_ref[:, hs] = o_ref[h].T.astype(BF16)
            g = dot(own_t, ds, NN)
            for b in range(REACH - count, REACH):
                g = g + dot(kt[b][...], ds_ref[h, b * rows : (b + 1) * rows, :], NN)
            dq_ref[:, hs] = (g * (st_ref[h, 1:2, :] * factor)).T.astype(BF16)
            x = dot(ds, q_low[h], NN)
            y = dot(p, do_low[h], NN)
            dk = x if h == 0 else dk + x
            dv = y if h == 0 else dv + y
        mine_ref[0:rows, :] = dk * factor
        mine_ref[rows:, :] = dv

    by_count(begin_ref, run)


def call(kernel, name, outs, scratch, vmem, flops, *args, in_hbm=0):
    vm = pl.BlockSpec(memory_space=pltpu.VMEM)
    hbm = pl.BlockSpec(memory_space=pltpu.HBM)
    moved = sum(math.prod(a.shape) * a.dtype.itemsize for a in args)
    return pl.pallas_call(
        kernel,
        out_shape=[jax.ShapeDtypeStruct(*o) for o in outs],
        in_specs=[hbm] * in_hbm + [vm] * (len(args) - in_hbm),
        out_specs=[vm] * len(outs),
        scratch_shapes=[pltpu.VMEM(*s) if isinstance(s, tuple) else s for s in scratch],
        compiler_params=pltpu.CompilerParams(vmem_limit_bytes=int(vmem * 2**20)),
        cost_estimate=pl.CostEstimate(flops=flops, bytes_accessed=moved, transcendentals=0),
        name=name,
    )(*(pltpu.with_memory_space_constraint(a, pltpu.HBM) for a in args[:in_hbm]), *args[in_hbm:])


def stage(k, v):
    rows, hd = k.shape
    return call(
        stage_kernel, "stage", [((2 * rows, hd), BF16)], [pltpu.SemaphoreType.DMA((2,))],
        STAGE_MB, 0, k, v, in_hbm=2,
    )[0]


def attention_grads(lens, q, do, packed, far, first_of):
    rows, hd = packed.shape[0] // 2, packed.shape[1]
    heads = q.shape[1] // hd
    width = REACH * rows
    block = 2 * heads * rows * rows * hd
    stack = ((heads, rows, hd), BF16)
    tall = (heads, hd, rows)
    line = ((heads, 1, rows), F32)
    square = (heads, rows, rows)
    qs, dos, dot_t, begin, s_own, dp_own, m_own, l_own, o_own = call(
        functools.partial(local_kernel, first_of=first_of),
        "local",
        [stack, stack, (tall, BF16), ((1, rows), jnp.int32), (square, F32), (square, F32), line, line, (tall, F32)],
        [((1, lens.shape[0]), jnp.int32), (q.shape, BF16), (do.shape, BF16), pltpu.SemaphoreType.DMA((3,))],
        16, 3 * block, lens.reshape(1, -1), q, do, packed, in_hbm=3,
    )
    scored = [
        call(
            functools.partial(score_kernel, distance=REACH - b),
            "score",
            [(square, F32), (square, F32), ((heads, 8, rows), F32), ((hd, rows), BF16), ((hd + 8, rows), BF16)],
            [], 12, 2 * block, qs, dos, begin, far[b],
        )
        for b in range(1, REACH)
    ]
    s, dp, m, kt, vt = zip(*scored)
    *back, ds, o, st, q_low, do_low, kt_far = call(
        remote_kernel,
        "remote",
        [((2 * rows, hd), BF16)] * REACH
        + [((heads, width, rows), BF16), (tall, F32), ((heads, 3, rows), F32), stack, stack, ((hd, rows), BF16)],
        [((heads, width, rows), BF16), (square, F32), (square, F32), ((heads, 8, rows), F32), ((hd + 8, rows), BF16)],
        24, 12 * block, begin, far[0], qs, dos, dot_t, m_own, l_own, o_own, *s, *dp, *m, *vt,
    )
    return back, lambda: call(
        own_kernel,
        "own",
        [(q.shape, BF16)] * 2 + [((2 * rows, hd), F32)],
        [],
        12, 7 * block, begin, q_low, do_low, s_own, dp_own, st, o, ds, packed, kt_far, *kt,
    )


def shifted(block, distance):
    count = lax.axis_size("ctx") * lax.axis_size("grp")
    route = [(i, (i + distance) % count) for i in range(count)]
    return lax.ppermute(block, ("ctx", "grp"), route)


def body(queries, key_rows, value_rows, out_grad, doc_lengths):
    rows, hd = key_rows.shape

    def first_of():
        return (lax.axis_index("ctx") * lax.axis_size("grp") + lax.axis_index("grp")) * rows

    packed = stage(key_rows, value_rows)
    far = [shifted(packed, d) for d in range(REACH, 0, -1)]
    back, finish = attention_grads(
        doc_lengths, queries, out_grad, packed, far, first_of
    )
    came = [shifted(back[REACH - d], -d) for d in (2, 3, 1, 4)]
    attended, query_grad, total = finish()
    for part in came:
        total = total + part.astype(F32)
    total = total.astype(BF16)
    return attended, query_grad, total[:rows], total[rows:]


def solution(mesh):
    split = P(("ctx", "grp"), None)
    return jax.shard_map(
        body, mesh=mesh, in_specs=(split,) * 4 + (P(),), out_specs=(split,) * 4, check_vma=False
    )
```

```python
import functools
import math

import jax
import jax.numpy as jnp
from jax import lax
from jax.experimental import pallas as pl
from jax.experimental.pallas import tpu as pltpu
from jax.sharding import PartitionSpec as P

F32, BF16 = jnp.float32, jnp.bfloat16
NT = (((1,), (1,)), ((), ()))
NN = (((1,), (0,)), ((), ()))
LOG2E = 1.4426950408889634
REACH = 4
CHUNK = 64
STAGE_MB = 16


def dot(a, b, dims):
    return lax.dot_general(a, b, dims, preferred_element_type=F32)


def fold(x, op):
    return op(x.reshape(x.shape[0] // 8, 8, x.shape[1]), axis=0)


def stage_kernel(k_hbm, v_hbm, packed, sem):
    rows = k_hbm.shape[0]
    copies = [
        pltpu.make_async_copy(k_hbm, packed.at[0:rows, :], sem.at[0]),
        pltpu.make_async_copy(v_hbm, packed.at[rows : 2 * rows, :], sem.at[1]),
    ]
    for c in copies:
        c.start()
    for c in copies:
        c.wait()


def local_kernel(
    lens_hbm, q_hbm, do_hbm, kv_ref, qs, dos, dot_t, reach_ref, s_own, dp_own, m_own, l_own, o_own,
    lens_ref, q_ref, do_ref, sem, *, first_of
):
    heads, rows, hd = qs.shape
    scale = LOG2E / math.sqrt(hd)
    copies = [
        pltpu.make_async_copy(src, dst, sem.at[i])
        for i, (src, dst) in enumerate(((lens_hbm, lens_ref), (q_hbm, q_ref), (do_hbm, do_ref)))
    ]
    for c in copies:
        c.start()
    copies[0].wait()
    q0 = first_of()
    nd = lens_ref.shape[1]
    lens = lens_ref[...]
    di = lax.broadcasted_iota(jnp.int32, (nd, nd), 0)
    dj = lax.broadcasted_iota(jnp.int32, (nd, nd), 1)
    ends = jnp.sum(jnp.where(dj <= di, lens, 0), axis=1, keepdims=True)
    length = jnp.sum(jnp.where(dj == di, lens, 0), axis=1, keepdims=True)
    qpos = lax.broadcasted_iota(jnp.int32, (1, rows), 1)
    begin = jnp.sum(jnp.where(ends <= qpos + q0, length, 0), axis=0, keepdims=True) - q0
    reach_ref[...] = begin
    kpos = lax.broadcasted_iota(jnp.int32, (rows, 1), 0)
    hide = jnp.where((kpos >= begin) & (kpos <= qpos), 0.0, -jnp.inf)
    vt = kv_ref[rows:, :].T
    copies[1].wait()
    copies[2].wait()
    for h in range(heads):
        q = q_ref[:, h * hd : (h + 1) * hd]
        do = do_ref[:, h * hd : (h + 1) * hd]
        qs[h] = q
        dos[h] = do
        dot_t[h] = do.T
        s = dot(kv_ref[0:rows, :], q, NT) * scale + hide
        m = jnp.max(fold(s, jnp.max), axis=0, keepdims=True)
        p = jnp.exp2(s - m)
        s_own[h] = s
        dp_own[h] = dot(kv_ref[rows:, :], do, NT)
        m_own[h] = m
        l_own[h] = jnp.sum(fold(p, jnp.sum), axis=0, keepdims=True)
        o_own[h] = dot(vt, p.astype(BF16), NN)


def score_block(q_ref, do_ref, begin, kv_ref, s_out, dp_out, m_out, distance):
    heads, rows, hd = q_ref.shape
    scale = LOG2E / math.sqrt(hd)
    kpos = lax.broadcasted_iota(jnp.int32, (rows, 1), 0) - distance * rows
    hide = jnp.where(kpos >= begin, 0.0, -jnp.inf)
    for h in range(heads):
        s = dot(kv_ref[0:rows, :], q_ref[h], NT) * scale + hide
        s_out[h] = s
        m_out[h] = fold(s, jnp.max)
        dp_out[h] = dot(kv_ref[rows:, :], do_ref[h], NT)


def turned(kv_ref, kt_out, vt_out):
    rows, hd = kv_ref.shape[0] // 2, kv_ref.shape[1]
    kt_out[...] = kv_ref[0:rows, :].T
    vt_out[0:hd, :] = kv_ref[rows:, :].T
    vt_out[hd:, :] = jnp.ones((vt_out.shape[0] - hd, rows), BF16)


def score_kernel(q_ref, do_ref, begin_ref, kv_ref, s_out, dp_out, m_out, kt_out, vt_out, *, distance):
    rows = begin_ref.shape[1]
    turned(kv_ref, kt_out, vt_out)

    @pl.when(jnp.min(begin_ref[...]) < (1 - distance) * rows)
    def _():
        score_block(q_ref, do_ref, begin_ref[...], kv_ref, s_out, dp_out, m_out, distance)


def far_blocks(count, q_ref, do_ref, dot_t, m_own, l_own, o_own, *refs):
    s_in, dp_in, m_in, vt, back = [refs[i * REACH : (i + 1) * REACH] for i in range(5)]
    ds_out, o_out, st_out, q_low, do_low, p_buf = refs[5 * REACH :]
    heads, rows, hd = q_ref.shape
    factor = 1.0 / math.sqrt(hd)
    seen = range(REACH - count, REACH)
    tiles = [(b, slice(c, c + CHUNK)) for b in seen for c in range(0, rows, CHUNK)]
    def weights(h):
        m = m_own[h]
        for b in seen:
            m = jnp.maximum(m, jnp.max(m_in[b][h], axis=0, keepdims=True))
        st_out[h, 0:1, :] = m
        for b, cs in tiles:
            at = slice(b * rows + cs.start, b * rows + cs.stop)
            p_buf[h, at, :] = jnp.exp2(s_in[b][h, cs, :] - m).astype(BF16)

    def output(h):
        w = jnp.exp2(m_own[h] - st_out[h, 0:1, :])
        total = w * l_own[h]
        o = w * o_own[h]
        if count:
            far_o = sum(dot(vt[b][...], p_buf[h, b * rows : (b + 1) * rows, :], NN) for b in seen)
            total = total + far_o[hd : hd + 1, :]
            o = o + far_o[0:hd, :]
        inv = 1.0 / total
        o = o * inv
        o_out[h] = o
        st_out[h, 1:2, :] = inv
        st_out[h, 2:3, :] = jnp.sum(fold(o * dot_t[h].astype(F32), jnp.sum), axis=0, keepdims=True)

    def scaled(h):
        col = jnp.broadcast_to(st_out[h, 1:2, :], (8, rows)).T[:, 0:1]
        q_low[h] = (q_ref[h].astype(F32) * col).astype(BF16)
        do_low[h] = (do_ref[h].astype(F32) * col).astype(BF16)

    def slopes(h):
        delta = st_out[h, 2:3, :]
        for b, cs in tiles:
            at = slice(b * rows + cs.start, b * rows + cs.stop)
            ds_out[h, at, :] = p_buf[h, at, :] * (dp_in[b][h, cs, :] - delta).astype(BF16)

    low = (REACH - count) * rows
    if low:
        ds_out[:, 0:low, :] = jnp.zeros((heads, low, rows), BF16)
    for b in range(REACH - count):
        back[b][...] = jnp.zeros(back[b].shape, BF16)

    def prepare(hs):
        for h in hs:
            weights(h)
        for h in hs:
            output(h)
        for h in hs:
            scaled(h)
            slopes(h)

    def grads(hs):
        dk = dv = None
        for h in hs:
            x = dot(ds_out[h, low:, :], q_low[h], NN)
            y = dot(p_buf[h, low:, :], do_low[h], NN)
            dk = x if dk is None else dk + x
            dv = y if dv is None else dv + y
        return dk, dv

    group = 2
    sets = [range(g, g + group) for g in range(0, heads, group)]
    parts = []
    for g, hs in enumerate(sets):
        prepare(hs)
        if count and g:
            parts.append(grads(sets[g - 1]))
    if not count:
        return
    parts.append(grads(sets[-1]))
    dk = sum(p[0] for p in parts)
    dv = sum(p[1] for p in parts)
    for i, b in enumerate(seen):
        bs = slice(i * rows, (i + 1) * rows)
        back[b][0:rows, :] = (dk[bs, :] * factor).astype(BF16)
        back[b][rows:, :] = dv[bs, :].astype(BF16)


def by_count(begin_ref, run):
    first = jnp.min(begin_ref[...])
    rows = begin_ref.shape[1]
    for count in range(REACH + 1):
        near = first < (1 - count) * rows if count else first >= 0
        far = first >= -count * rows if count < REACH else first < (1 - REACH) * rows

        @pl.when(near & far)
        def _(count=count):
            run(count)


def remote_kernel(begin_ref, kv_ref, q_ref, do_ref, dot_t, m_own, l_own, o_own, *refs):
    near = REACH - 1
    s_in, dp_in, m_in, vt = [refs[i * near : (i + 1) * near] for i in range(4)]
    *outs, kt_out, p_buf, s_far, dp_far, m_far, vt_far = refs[4 * near :]

    def run(count):
        turned(kv_ref, kt_out, vt_far)
        if count == REACH:
            score_block(q_ref, do_ref, begin_ref[...], kv_ref, s_far, dp_far, m_far, REACH)
        far_blocks(
            count, q_ref, do_ref, dot_t, m_own, l_own, o_own,
            s_far, *s_in, dp_far, *dp_in, m_far, *m_in, vt_far, *vt, *outs, p_buf,
        )

    by_count(begin_ref, run)


def own_kernel(q_low, do_low, s_own, dp_own, st_ref, o_ref, ds_ref, kv_ref, *refs):
    far_kt = refs[:REACH]
    out_ref, dq_ref, mine_ref, kt = refs[REACH:]
    heads, hd, rows = o_ref.shape
    factor = 1.0 / math.sqrt(hd)
    own_t = kv_ref[0:rows, :].T
    for b in range(REACH):
        kt[:, b * rows : (b + 1) * rows] = far_kt[b][...]
    dk = dv = None
    for h in range(heads):
        hs = slice(h * hd, (h + 1) * hd)
        p = jnp.exp2(s_own[h] - st_ref[h, 0:1, :]).astype(BF16)
        ds = p * (dp_own[h] - st_ref[h, 2:3, :]).astype(BF16)
        out_ref[:, hs] = o_ref[h].T.astype(BF16)
        g = dot(kt[...], ds_ref[h], NN) + dot(own_t, ds, NN)
        dq_ref[:, hs] = (g * (st_ref[h, 1:2, :] * factor)).T.astype(BF16)
        x = dot(ds, q_low[h], NN)
        y = dot(p, do_low[h], NN)
        dk = x if h == 0 else dk + x
        dv = y if h == 0 else dv + y
    mine_ref[0:rows, :] = dk * factor
    mine_ref[rows:, :] = dv


def call(kernel, name, outs, scratch, vmem, flops, *args, in_hbm=0):
    vm = pl.BlockSpec(memory_space=pltpu.VMEM)
    hbm = pl.BlockSpec(memory_space=pltpu.HBM)
    moved = sum(math.prod(a.shape) * a.dtype.itemsize for a in args)
    return pl.pallas_call(
        kernel,
        out_shape=[jax.ShapeDtypeStruct(*o) for o in outs],
        in_specs=[hbm] * in_hbm + [vm] * (len(args) - in_hbm),
        out_specs=[vm] * len(outs),
        scratch_shapes=[pltpu.VMEM(*s) if isinstance(s, tuple) else s for s in scratch],
        compiler_params=pltpu.CompilerParams(vmem_limit_bytes=int(vmem * 2**20)),
        cost_estimate=pl.CostEstimate(flops=flops, bytes_accessed=moved, transcendentals=0),
        name=name,
    )(*(pltpu.with_memory_space_constraint(a, pltpu.HBM) for a in args[:in_hbm]), *args[in_hbm:])


def stage(k, v):
    rows, hd = k.shape
    return call(
        stage_kernel, "stage", [((2 * rows, hd), BF16)], [pltpu.SemaphoreType.DMA((2,))],
        STAGE_MB, 0, k, v, in_hbm=2,
    )[0]


def attention_grads(lens, q, do, packed, far, first_of):
    rows, hd = packed.shape[0] // 2, packed.shape[1]
    heads = q.shape[1] // hd
    width = REACH * rows
    block = 2 * heads * rows * rows * hd
    stack = ((heads, rows, hd), BF16)
    tall = (heads, hd, rows)
    line = ((heads, 1, rows), F32)
    square = (heads, rows, rows)
    qs, dos, dot_t, begin, s_own, dp_own, m_own, l_own, o_own = call(
        functools.partial(local_kernel, first_of=first_of),
        "local",
        [stack, stack, (tall, BF16), ((1, rows), jnp.int32), (square, F32), (square, F32), line, line, (tall, F32)],
        [((1, lens.shape[0]), jnp.int32), (q.shape, BF16), (do.shape, BF16), pltpu.SemaphoreType.DMA((3,))],
        16, 3 * block, lens.reshape(1, -1), q, do, packed, in_hbm=3,
    )
    scored = [
        call(
            functools.partial(score_kernel, distance=REACH - b),
            "score",
            [(square, F32), (square, F32), ((heads, 8, rows), F32), ((hd, rows), BF16), ((hd + 8, rows), BF16)],
            [], 12, 2 * block, qs, dos, begin, far[b],
        )
        for b in range(1, REACH)
    ]
    s, dp, m, kt, vt = zip(*scored)
    *back, ds, o, st, q_low, do_low, kt_far = call(
        remote_kernel,
        "remote",
        [((2 * rows, hd), BF16)] * REACH
        + [((heads, width, rows), BF16), (tall, F32), ((heads, 3, rows), F32), stack, stack, ((hd, rows), BF16)],
        [((heads, width, rows), BF16), (square, F32), (square, F32), ((heads, 8, rows), F32), ((hd + 8, rows), BF16)],
        24, 12 * block, begin, far[0], qs, dos, dot_t, m_own, l_own, o_own, *s, *dp, *m, *vt,
    )
    return back, lambda: call(
        own_kernel,
        "own",
        [(q.shape, BF16)] * 2 + [((2 * rows, hd), F32)],
        [((hd, width), BF16)],
        12, 7 * block, q_low, do_low, s_own, dp_own, st, o, ds, packed, kt_far, *kt,
    )


def shifted(block, distance):
    count = lax.axis_size("ctx") * lax.axis_size("grp")
    route = [(i, (i + distance) % count) for i in range(count)]
    return lax.ppermute(block, ("ctx", "grp"), route)


def body(queries, key_rows, value_rows, out_grad, doc_lengths):
    rows, hd = key_rows.shape

    def first_of():
        return (lax.axis_index("ctx") * lax.axis_size("grp") + lax.axis_index("grp")) * rows

    packed = stage(key_rows, value_rows)
    far = [shifted(packed, d) for d in range(REACH, 0, -1)]
    back, finish = attention_grads(
        doc_lengths, queries, out_grad, packed, far, first_of
    )
    came = [shifted(back[REACH - d], -d) for d in range(1, REACH + 1)]
    attended, query_grad, total = finish()
    for part in came:
        total = total + part.astype(F32)
    total = total.astype(BF16)
    return attended, query_grad, total[:rows], total[rows:]


def solution(mesh):
    split = P(("ctx", "grp"), None)
    return jax.shard_map(
        body, mesh=mesh, in_specs=(split,) * 4 + (P(),), out_specs=(split,) * 4, check_vma=False
    )
```
